512 devices in a mesh: grp: 2 (over core), row: 16 (over y, x_hi), col: 16 (over x_lo, z).
Axes of the slice: x: 4 (x_hi: 2, x_lo: 2; x = x_hi * 2 + x_lo), y: 8, z: 8, core: 2. Of those that a mesh axis runs over, the one named last changes fastest.
Arguments:
- density: float32 [256, 256, 256], P(('grp', 'row'), 'col'), may hold values from -8 to 8
- kernel_hat: float32 [512, 512, 512], P(('grp', 'row'), 'col'), may hold values from 0 to 8193, as said below
Outputs:
- potential: float32 [256, 256, 256], P(('grp', 'row'), 'col')
The draws below stay inside these ranges and needn't reach their ends.
Inputs may be any that keep to these rules, and one draw needn't show every extreme that they name: kernel_hat[b, c, a] is unchanged when any one of its three indices i is replaced by (512 - i) mod 512.
All inputs are finite; a program needn't handle non-finite values.
Results may differ from the reference program's by a relative error of at most 0.000051.
Values sent between devices are 32-bit elements; how exact they have to be, the bound alone decides.
No kernel may reach another device: no remote copies, remote signals or barrier semaphores. Data moves between devices by JAX's collectives and lax.ppermute only.
A program may use at most 64 MiB of HBM per device.

```python
import jax
import jax.numpy as jnp

M = 256
L = 512


def draw_density(key, part):
    key = jax.random.fold_in(key, 11)
    values = jax.random.normal(key, (M, M, M), jnp.float32)
    return jnp.clip(values, -8.0, 8.0)


def draw_kernel_hat(key, part):
    key = jax.random.fold_in(key, 23)
    shape = (L, L, L)
    index_a = jax.lax.broadcasted_iota(jnp.int32, shape, 0)
    index_b = jax.lax.broadcasted_iota(jnp.int32, shape, 1)
    index_c = jax.lax.broadcasted_iota(jnp.int32, shape, 2)
    fold_ia = jnp.minimum(index_a, L - index_a)
    fold_ib = jnp.minimum(index_b, L - index_b)
    fold_ic = jnp.minimum(index_c, L - index_c)
    fold_a = fold_ia.astype(jnp.float32)
    fold_b = fold_ib.astype(jnp.float32)
    fold_c = fold_ic.astype(jnp.float32)
    wave_sq = fold_a * fold_a + fold_b * fold_b + fold_c * fold_c
    base = M * M // 16 / (wave_sq + 1.0) + 0.5
    small_shape = (M + 1, M + 1, M + 1)
    rough_small = jnp.exp(jax.random.uniform(key, small_shape, jnp.float32, -0.6931, 0.6931))
    rough = rough_small[fold_ia, fold_ib, fold_ic]
    return base * rough


def setup_inputs(seed: int = 0) -> dict:
    streams_of = jax.random.split(jax.random.key(seed), 3)
    return {
        "density": draw_density(jax.random.fold_in(streams_of[2], 71), 0),
        "kernel_hat": draw_kernel_hat(jax.random.fold_in(streams_of[2], 71), 0),
    }


def reference(density, kernel_hat):
    along_z = jnp.fft.fft(density, n=L, axis=2)
    along_y = jnp.fft.fft(along_z, n=L, axis=1)
    spectrum = jnp.fft.fft(along_y, n=L, axis=0)
    kernel = jnp.transpose(kernel_hat, (2, 0, 1))
    product = spectrum * kernel
    back_x = jnp.fft.ifft(product, axis=0)[:M]
    back_y = jnp.fft.ifft(back_x, axis=1)[:, :M]
    back_z = jnp.fft.ifft(back_y, axis=2)[:, :, :M]
    return jnp.real(back_z).astype(jnp.float32)
```

```python
import functools

import jax
import jax.numpy as jnp
import ml_dtypes
import numpy as np
from jax import lax
from jax.experimental import pallas as pl
from jax.experimental.pallas import tpu as pltpu
from jax.sharding import PartitionSpec as P


GA = ("grp", "row")
ALL = ("col", "grp", "row")
NN = (((1,), (0,)), ((), ()))
NT = (((1,), (1,)), ((), ()))
VMEM = pl.BlockSpec(memory_space=pltpu.VMEM)


def modes(freqs_c, freqs_s, cells, length):
    centre = np.arange(cells) - (cells - 1) / 2.0
    angle = 2.0 * np.pi / length
    return np.concatenate(
        [np.cos(angle * np.outer(freqs_c, centre)), np.sin(angle * np.outer(freqs_s, centre))], 0
    )


def halves(table):
    table = np.asarray(table, np.float32)
    hi = table.astype(ml_dtypes.bfloat16)
    lo = (table - hi.astype(np.float32)).astype(ml_dtypes.bfloat16)
    return jnp.asarray(hi), jnp.asarray(lo)


def split(x):
    hi = x.astype(jnp.bfloat16)
    return hi, (x - hi.astype(jnp.float32)).astype(jnp.bfloat16)


def dot3(left, right, dims):
    one = functools.partial(lax.dot_general, dimension_numbers=dims, preferred_element_type=jnp.float32)
    return one(left[0], right[0]) + (one(left[0], right[1]) + one(left[1], right[0]))


def exchange_blocks(v, block):
    count, lanes = len(v), v[0].shape[1]
    lane_block = lax.broadcasted_iota(jnp.int32, v[0].shape, 1) // block
    step = 1
    while step < count:
        odd = (lane_block & step) != 0
        w = list(v)
        for n in range(count):
            if n & step == 0:
                low, high = v[n], v[n + step]
                w[n] = jnp.where(odd, pltpu.roll(high, step * block, 1), low)
                w[n + step] = jnp.where(odd, high, pltpu.roll(low, lanes - step * block, 1))
        v = w
        step *= 2
    return v


def forward_z(d_ref, th_ref, tl_ref, out_ref):
    d = d_ref[...]
    d = d.reshape(d.shape[0] * d.shape[1], d.shape[2])
    out_ref[...] = dot3((th_ref[...], tl_ref[...]), split(d), NT)


def pick_kernel(k_ref, out_ref, *, blocks_a, half):
    index = lax.axis_index("grp") * lax.axis_size("row") + lax.axis_index("row")
    first = jnp.where(index >= blocks_a // 2, 1, 0)
    rows = out_ref.shape[1]
    edge = k_ref[0]
    pieces = []
    for t in range(half // 64 + 1):
        tile = edge[:, t // 2 * 128 : t // 2 * 128 + 128]
        pieces.append(tile if t % 2 else pltpu.roll(tile, 64, 1))
    for s in range(rows):
        row = k_ref[first + s]
        out_ref[:, s, :half] = row[:, :half]
        last = row[:, half:]
        if s < len(pieces):
            lane = lax.broadcasted_iota(jnp.int32, last.shape, 1)
            last = jnp.where(lane < 64, last, pieces[s])
        out_ref[:, s, half:] = last


def convolve(r_ref, k_ref, bh_ref, bl_ref, ah_ref, al_ref, out_ref, *, blocks_a, blocks_b, slab_x, slab_y):
    cells = blocks_b * slab_y
    half = cells
    per = slab_x
    groups = []
    for h in range(blocks_b // per):
        v = [r_ref[(h * per + n) * blocks_a : (h * per + n + 1) * blocks_a, :] for n in range(per)]
        groups.append(jnp.concatenate(exchange_blocks(v, slab_y), 0))
    r = jnp.concatenate(groups, 1)
    tb = (bh_ref[...], bl_ref[...])
    ta = (ah_ref[...], al_ref[...])
    p = dot3(tb, split(r), NT)
    q = dot3(split(p), ta, NN)
    k = k_ref[...]
    k = k.reshape(k.shape[0] * k.shape[1], k.shape[2])
    main = k[:, :half]
    column = k[:, half : half + 1]
    tile = k_ref[blocks_a // 2][:, half:]
    lane = lax.broadcasted_iota(jnp.int32, (1, 128), 1)
    parts = []
    for t in range(0, half // 64, 2):
        parts.append(jnp.where(lane < 64, pltpu.roll(tile[t : t + 1], 64, 1), tile[t + 1 : t + 2]))
    row = jnp.concatenate(parts, 1)
    corner = tile[half // 64 : half // 64 + 1, 64:65]
    row_id = lax.broadcasted_iota(jnp.int32, main.shape, 0)
    lane_id = lax.broadcasted_iota(jnp.int32, main.shape, 1)
    first_row, first_lane = row_id == 0, lane_id == 0
    scale = jnp.where(first_row, 0.5, 1.0) * jnp.where(first_lane, 0.5, 1.0) * (1.0 / (half * half))
    cc = main
    cs = jnp.where(first_lane, column, main)
    sc = jnp.where(first_row, row, main)
    ss = jnp.where(first_lane, column, main)
    ss = jnp.where(first_row, jnp.where(first_lane, corner, row), ss)
    kk = jnp.concatenate(
        [jnp.concatenate([cc * scale, cs * scale], 1), jnp.concatenate([sc * scale, ss * scale], 1)], 0
    )
    w = dot3(ta, split(q * kk), NT)
    v = dot3(split(w), tb, NN)
    for h in range(blocks_b // per):
        lanes = slice(h * per * slab_y, (h + 1) * per * slab_y)
        v_h = exchange_blocks([v[n * blocks_a : (n + 1) * blocks_a, lanes] for n in range(per)], slab_y)
        for n in range(per):
            out_ref[(h * per + n) * blocks_a : (h * per + n + 1) * blocks_a, :] = v_h[n]


def inverse_z(r_ref, th_ref, tl_ref, out_ref):
    r = r_ref[...]
    modes_c = r.shape[0] // 2
    row_id = lax.broadcasted_iota(jnp.int32, r.shape, 0)
    r = r * jnp.where(row_id % modes_c == 0, 0.5 / modes_c, 1.0 / modes_c)
    out = dot3(split(r.T), (th_ref[...], tl_ref[...]), NN)
    out_ref[...] = out.reshape(out_ref.shape)


def call(kernel, shape, operands, flops):
    size = sum(x.size * x.dtype.itemsize for x in operands) + 4 * int(np.prod(shape))
    return pl.pallas_call(
        kernel,
        out_shape=jax.ShapeDtypeStruct(shape, jnp.float32),
        in_specs=[VMEM] * len(operands),
        out_specs=VMEM,
        compiler_params=pltpu.CompilerParams(vmem_limit_bytes=40 * 1024 * 1024),
        cost_estimate=pl.CostEstimate(flops=flops, bytes_accessed=size, transcendentals=0),
    )(*operands)


def body(density, kernel_hat):
    blocks_a = lax.axis_size(GA)
    blocks_b = lax.axis_size("col")
    slab_x, slab_y, cells = density.shape
    length = 2 * cells
    per_b, per_c = kernel_hat.shape[:2]

    tz = halves(modes(np.arange(cells), cells - np.arange(cells), cells, length))
    owner, sub = np.divmod(np.arange(cells), cells // blocks_a)
    order_b = np.where(owner < blocks_a // 2, per_b * owner + sub, length - 1 - per_b * owner - sub)
    tb = halves(modes(order_b, np.where(order_b == 0, cells, order_b), cells, length))
    order_a = np.arange(cells)
    order_x = np.arange(cells).reshape(blocks_a, slab_x).T.reshape(-1)
    ta = halves(modes(order_a, np.where(order_a == 0, cells, order_a), cells, length)[:, order_x].T)

    picked = pl.pallas_call(
        functools.partial(pick_kernel, blocks_a=blocks_a, half=cells),
        grid=(1,),
        out_shape=jax.ShapeDtypeStruct((per_c, cells // blocks_a, cells + 128), jnp.float32),
        in_specs=[pl.BlockSpec((cells // blocks_a + 1, per_c, cells + 128), lambda i: (0, 0, 0))],
        out_specs=pl.BlockSpec((per_c, cells // blocks_a, cells + 128), lambda i: (0, 0, 0)),
        cost_estimate=pl.CostEstimate(flops=0, bytes_accessed=8 * 32 * 8 * 384, transcendentals=0),
    )(kernel_hat)
    kernel = lax.all_to_all(picked, GA, split_axis=0, concat_axis=0, tiled=True)

    sent = call(forward_z, (length, slab_x * slab_y), (density, *tz), 6 * 128 * 256 * 512)
    got = lax.all_to_all(sent, ALL, split_axis=0, concat_axis=0, tiled=True)
    sizes = dict(blocks_a=blocks_a, blocks_b=blocks_b, slab_x=slab_x, slab_y=slab_y)
    back = call(
        functools.partial(convolve, **sizes),
        (length, slab_x * slab_y),
        (got, kernel, *tb, *ta),
        6 * 200 * 10**6,
    )
    got = lax.all_to_all(back, ALL, split_axis=0, concat_axis=0, tiled=True)
    return call(inverse_z, density.shape, (got, *tz), 6 * 128 * 256 * 512)


def solution(mesh):
    return jax.shard_map(
        body,
        mesh=mesh,
        in_specs=(P(GA, "col", None), P(GA, "col", None)),
        out_specs=P(GA, "col", None),
        check_vma=False,
    )
```

```python
import functools

import jax
import jax.numpy as jnp
import ml_dtypes
import numpy as np
from jax import lax
from jax.experimental import pallas as pl
from jax.experimental.pallas import tpu as pltpu
from jax.sharding import PartitionSpec as P


GA = ("grp", "row")
ALL = ("col", "grp", "row")
NN = (((1,), (0,)), ((), ()))
NT = (((1,), (1,)), ((), ()))
VMEM = pl.BlockSpec(memory_space=pltpu.VMEM)


def modes(freqs_c, freqs_s, cells, length):
    centre = np.arange(cells) - (cells - 1) / 2.0
    angle = 2.0 * np.pi / length
    return np.concatenate(
        [np.cos(angle * np.outer(freqs_c, centre)), np.sin(angle * np.outer(freqs_s, centre))], 0
    )


def halves(table):
    table = np.asarray(table, np.float32)
    hi = table.astype(ml_dtypes.bfloat16)
    lo = (table - hi.astype(np.float32)).astype(ml_dtypes.bfloat16)
    return jnp.asarray(np.stack([hi, lo]))


def split(x):
    hi = x.astype(jnp.bfloat16)
    return hi, (x - hi.astype(jnp.float32)).astype(jnp.bfloat16)


def dot3(left, right, dims):
    one = functools.partial(lax.dot_general, dimension_numbers=dims, preferred_element_type=jnp.float32)
    return one(left[0], right[0]) + (one(left[0], right[1]) + one(left[1], right[0]))


def exchange_blocks(v, block):
    count, lanes = len(v), v[0].shape[1]
    lane_block = lax.broadcasted_iota(jnp.int32, v[0].shape, 1) // block
    step = 1
    while step < count:
        odd = (lane_block & step) != 0
        w = list(v)
        for n in range(count):
            if n & step == 0:
                low, high = v[n], v[n + step]
                w[n] = jnp.where(odd, pltpu.roll(high, step * block, 1), low)
                w[n + step] = jnp.where(odd, high, pltpu.roll(low, lanes - step * block, 1))
        v = w
        step *= 2
    return v


def forward_z(d_hbm, t_hbm, out_ref, d_ref, t_ref, sems):
    copies = [
        pltpu.make_async_copy(t_hbm, t_ref, sems.at[0]),
        pltpu.make_async_copy(d_hbm, d_ref, sems.at[1]),
    ]
    for copy in copies:
        copy.start()
    for copy in copies:
        copy.wait()
    d = d_ref[...]
    d = d.reshape(d.shape[0] * d.shape[1], d.shape[2])
    out_ref[...] = dot3((t_ref[0], t_ref[1]), split(d), NT)


def pick_kernel(k_ref, out_ref, *, blocks_a, half):
    index = lax.axis_index("grp") * lax.axis_size("row") + lax.axis_index("row")
    first = jnp.where(index >= blocks_a // 2, 1, 0)
    rows, tiles = half // blocks_a, half // 128
    per = k_ref.shape[1]
    edge = k_ref[0]
    lane = lax.broadcasted_iota(jnp.int32, (per, 128), 1)
    last = pltpu.roll(edge[:, half:], rows, 1)
    for s in range(rows):
        row = k_ref[first + s]
        for h in range(tiles):
            t = s * tiles + h
            out_ref[t * per : (t + 1) * per, :] = row[:, h * 128 : (h + 1) * 128]
        column = row[:, half:]
        last = jnp.where(lane == s, pltpu.roll(column, s, 1) if s else column, last)
    for h in range(tiles):
        t = rows * tiles + h
        out_ref[t * per : (t + 1) * per, :] = edge[:, h * 128 : (h + 1) * 128]
    t = (rows + 1) * tiles
    out_ref[t * per : (t + 1) * per, :] = last


def pack(r_ref, k_ref, out_ref, *, blocks_a, blocks_b, slab_x, slab_y):
    total = out_ref.shape[0] // blocks_a
    for h in range(blocks_b // slab_x):
        first = h * slab_x * blocks_a
        v = [r_ref[first + n * blocks_a : first + (n + 1) * blocks_a, :] for n in range(slab_x)]
        v = exchange_blocks(v, slab_y)
        for n in range(slab_x):
            out_ref[pl.ds(h * slab_x + n, blocks_a, stride=total), :] = v[n]
    for t in range(blocks_b, total):
        n = t - blocks_b
        out_ref[pl.ds(t, blocks_a, stride=total), :] = k_ref[n * blocks_a : (n + 1) * blocks_a, :]


def convolve(r_ref, b_ref, a_ref, out_ref, *, blocks_a, blocks_b, slab_x, slab_y):
    half = blocks_b * slab_y
    rows, tiles = half // blocks_a, half // 128
    total = r_ref.shape[0] // blocks_a
    per = slab_x

    def take(t):
        return r_ref[pl.ds(t, blocks_a, stride=total), :]

    r = jnp.concatenate(
        [jnp.concatenate([take(h * per + n) for n in range(per)], 0) for h in range(blocks_b // per)], 1
    )
    tb = (b_ref[0], b_ref[1])
    ta = (a_ref[0], a_ref[1])
    p = dot3(tb, split(r), NT)
    q = dot3(split(p), ta, NN)
    main = jnp.concatenate(
        [
            jnp.concatenate([take(blocks_b + s * tiles + h) for s in range(rows)], 0)
            for h in range(tiles)
        ],
        1,
    )
    tail = take(blocks_b + (rows + 1) * tiles)
    column = jnp.concatenate([tail[:, s : s + 1] for s in range(rows)], 0)
    edge = blocks_a // 2 * total + blocks_b + rows * tiles
    row = jnp.concatenate([r_ref[edge + h : edge + h + 1, :] for h in range(tiles)], 1)
    corner = r_ref[edge + tiles : edge + tiles + 1, rows : rows + 1]
    row_id = lax.broadcasted_iota(jnp.int32, main.shape, 0)
    lane_id = lax.broadcasted_iota(jnp.int32, main.shape, 1)
    first_row, first_lane = row_id == 0, lane_id == 0
    scale = jnp.where(first_row, 0.5, 1.0) * jnp.where(first_lane, 0.5, 1.0) * (1.0 / (half * half))
    cc = main
    cs = jnp.where(first_lane, column, main)
    sc = jnp.where(first_row, row, main)
    ss = jnp.where(first_row, jnp.where(first_lane, corner, row), cs)
    kk = jnp.concatenate(
        [jnp.concatenate([cc * scale, cs * scale], 1), jnp.concatenate([sc * scale, ss * scale], 1)], 0
    )
    w = dot3(ta, split(q * kk), NT)
    v = dot3(split(w), tb, NN)
    for h in range(blocks_b // per):
        lanes = slice(h * per * slab_y, (h + 1) * per * slab_y)
        v_h = exchange_blocks([v[n * blocks_a : (n + 1) * blocks_a, lanes] for n in range(per)], slab_y)
        for n in range(per):
            out_ref[(h * per + n) * blocks_a : (h * per + n + 1) * blocks_a, :] = v_h[n]


def inverse_z(r_ref, t_ref, out_ref):
    r = r_ref[...]
    modes_c = r.shape[0] // 2
    row_id = lax.broadcasted_iota(jnp.int32, r.shape, 0)
    r = r * jnp.where(row_id % modes_c == 0, 0.5 / modes_c, 1.0 / modes_c)
    out = dot3(split(r.T), (t_ref[0], t_ref[1]), NN)
    out_ref[...] = out.reshape(out_ref.shape)


def call(kernel, shape, operands, flops):
    size = sum(x.size * x.dtype.itemsize for x in operands) + 4 * int(np.prod(shape))
    return pl.pallas_call(
        kernel,
        out_shape=jax.ShapeDtypeStruct(shape, jnp.float32),
        in_specs=[VMEM] * len(operands),
        out_specs=VMEM,
        compiler_params=pltpu.CompilerParams(vmem_limit_bytes=40 * 1024 * 1024),
        cost_estimate=pl.CostEstimate(flops=flops, bytes_accessed=size, transcendentals=0),
    )(*operands)


def body(density, kernel_hat):
    blocks_a = lax.axis_size(GA)
    blocks_b = lax.axis_size("col")
    slab_x, slab_y, cells = density.shape
    length = 2 * cells
    per_b, per_c = kernel_hat.shape[:2]

    tz = halves(modes(np.arange(cells), cells - np.arange(cells), cells, length))
    sub, owner = np.divmod(np.arange(cells), blocks_a)
    order_b = np.where(owner < blocks_a // 2, per_b * owner + sub, length - 1 - per_b * owner - sub)
    tb = halves(modes(order_b, np.where(order_b == 0, cells, order_b), cells, length))
    order_a = np.arange(cells)
    order_x = np.arange(cells).reshape(blocks_a, slab_x).T.reshape(-1)
    ta = halves(modes(order_a, np.where(order_a == 0, cells, order_a), cells, length)[:, order_x].T)

    rows, tiles = cells // blocks_a, cells // 128
    extra = (rows + 1) * tiles + 1
    total = blocks_b + extra
    sizes = dict(blocks_a=blocks_a, blocks_b=blocks_b, slab_x=slab_x, slab_y=slab_y)
    picked = pl.pallas_call(
        functools.partial(pick_kernel, blocks_a=blocks_a, half=cells),
        grid=(1,),
        out_shape=jax.ShapeDtypeStruct((extra * per_c, 128), jnp.float32),
        in_specs=[pl.BlockSpec((rows + 1, per_c, cells + 128), lambda i: (0, 0, 0))],
        out_specs=VMEM,
        cost_estimate=pl.CostEstimate(flops=0, bytes_accessed=8 * 32 * 8 * 384, transcendentals=0),
    )(kernel_hat)

    sent = pl.pallas_call(
        forward_z,
        out_shape=jax.ShapeDtypeStruct((length, slab_x * slab_y), jnp.float32),
        in_specs=[pl.BlockSpec(memory_space=pltpu.HBM)] * 2,
        out_specs=VMEM,
        scratch_shapes=[
            pltpu.VMEM(density.shape, jnp.float32),
            pltpu.VMEM(tz.shape, jnp.bfloat16),
            pltpu.SemaphoreType.DMA((2,)),
        ],
        cost_estimate=pl.CostEstimate(flops=6 * 128 * 256 * 512, bytes_accessed=2**20, transcendentals=0),
    )(density, tz)
    got = lax.all_to_all(sent, "col", split_axis=0, concat_axis=0, tiled=True)
    packed = call(functools.partial(pack, **sizes), (blocks_a * total, 128), (got, picked), 0)
    got = lax.all_to_all(packed.reshape(blocks_a, 1, total * 128), GA, split_axis=0, concat_axis=0, tiled=True)
    back = call(
        functools.partial(convolve, **sizes),
        (length, slab_x * slab_y),
        (got.reshape(blocks_a * total, 128), tb, ta),
        6 * 200 * 10**6,
    )
    got = lax.all_to_all(back, ALL, split_axis=0, concat_axis=0, tiled=True)
    return call(inverse_z, density.shape, (got, tz), 6 * 128 * 256 * 512)


def solution(mesh):
    return jax.shard_map(
        body,
        mesh=mesh,
        in_specs=(P(GA, "col", None), P(GA, "col", None)),
        out_specs=P(GA, "col", None),
        check_vma=False,
    )
```

```python
import functools

import jax
import jax.numpy as jnp
import ml_dtypes
import numpy as np
from jax import lax
from jax.experimental import pallas as pl
from jax.experimental.pallas import tpu as pltpu
from jax.sharding import Mesh
from jax.sharding import PartitionSpec as P


GA = ("grp", "ra", "rb")
COL = ("ca", "cb")
RANKS = ("grp", "cb", "ra", "rb", "ca")
NN = (((1,), (0,)), ((), ()))
NT = (((1,), (1,)), ((), ()))
VMEM = pl.BlockSpec(memory_space=pltpu.VMEM)


def modes(freqs_c, freqs_s, cells, length):
    centre = np.arange(cells) - (cells - 1) / 2.0
    angle = 2.0 * np.pi / length
    return np.concatenate(
        [np.cos(angle * np.outer(freqs_c, centre)), np.sin(angle * np.outer(freqs_s, centre))], 0
    )


def halves(table):
    table = np.asarray(table, np.float32)
    hi = table.astype(ml_dtypes.bfloat16)
    lo = (table - hi.astype(np.float32)).astype(ml_dtypes.bfloat16)
    return jnp.asarray(np.stack([hi, lo]))


def split(x):
    hi = x.astype(jnp.bfloat16)
    return hi, (x - hi.astype(jnp.float32)).astype(jnp.bfloat16)


def dot3(left, right, dims):
    one = functools.partial(lax.dot_general, dimension_numbers=dims, preferred_element_type=jnp.float32)
    return one(left[0], right[0]) + (one(left[0], right[1]) + one(left[1], right[0]))


def exchange_blocks(v, block):
    count, lanes = len(v), v[0].shape[1]
    lane_block = lax.broadcasted_iota(jnp.int32, v[0].shape, 1) // block
    step = 1
    while step < count:
        odd = (lane_block & step) != 0
        w = list(v)
        for n in range(count):
            if n & step == 0:
                low, high = v[n], v[n + step]
                w[n] = jnp.where(odd, pltpu.roll(high, step * block, 1), low)
                w[n + step] = jnp.where(odd, high, pltpu.roll(low, lanes - step * block, 1))
        v = w
        step *= 2
    return v


def forward_z(d_hbm, t_hbm, out_ref, d_ref, t_ref, sems):
    copies = [
        pltpu.make_async_copy(t_hbm, t_ref, sems.at[0]),
        pltpu.make_async_copy(d_hbm, d_ref, sems.at[1]),
    ]
    for copy in copies:
        copy.start()
    for copy in copies:
        copy.wait()
    d = d_ref[...]
    d = d.reshape(d.shape[0] * d.shape[1], d.shape[2])
    out_ref[...] = dot3((t_ref[0], t_ref[1]), split(d), NT)


def pack(r_ref, k_ref, out_ref, *, blocks_a, blocks_b, slab_x, slab_y):
    half = blocks_b * slab_y
    rows, tiles = half // blocks_a, half // 128
    total = out_ref.shape[0] // blocks_a

    def put(t, value):
        out_ref[pl.ds(t, blocks_a, stride=total), :] = value

    for h in range(blocks_b // slab_x):
        first = h * slab_x * blocks_a
        v = [r_ref[first + n * blocks_a : first + (n + 1) * blocks_a, :] for n in range(slab_x)]
        v = exchange_blocks(v, slab_y)
        for n in range(slab_x):
            put(h * slab_x + n, v[n])
    first = lax.axis_index("grp")
    lane = lax.broadcasted_iota(jnp.int32, (blocks_a, 128), 1)
    last = pltpu.roll(k_ref[0, :, half : half + 128], rows, 1)
    for s in range(rows):
        for h in range(tiles):
            put(blocks_b + s * tiles + h, k_ref[first + s, :, h * 128 : (h + 1) * 128])
        column = k_ref[first + s, :, half : half + 128]
        last = jnp.where(lane == s, pltpu.roll(column, s, 1) if s else column, last)
    for h in range(tiles):
        put(blocks_b + rows * tiles + h, k_ref[0, :, h * 128 : (h + 1) * 128])
    put(blocks_b + (rows + 1) * tiles, last)


def convolve(r_ref, y_ref, x_ref, y_back_ref, x_back_ref, out_ref, *, blocks_a, blocks_b, slab_x, slab_y, runs):
    half = blocks_b * slab_y
    rows, tiles = half // blocks_a, half // 128
    total = r_ref.shape[0] // blocks_a
    per = slab_x

    def take(t):
        return r_ref[pl.ds(t, blocks_a, stride=total), :]

    r = jnp.concatenate(
        [jnp.concatenate([take(h * per + n) for n in range(per)], 0) for h in range(blocks_b // per)], 1
    )
    main = jnp.concatenate(
        [
            jnp.concatenate([take(blocks_b + s * tiles + h) for s in range(rows)], 0).T
            for h in range(tiles)
        ],
        0,
    )
    tail = take(blocks_b + (rows + 1) * tiles).T
    line = jnp.concatenate([tail[s : s + 1] for s in range(rows)], 1)
    edge = blocks_a // 2 * total + blocks_b + rows * tiles
    column = jnp.concatenate(
        [jnp.broadcast_to(r_ref[edge + h : edge + h + 1, :], (8, 128)).T[:, :1] for h in range(tiles)], 0
    )
    corner = r_ref[edge + tiles : edge + tiles + 1, rows : rows + 1]
    first_row = lax.broadcasted_iota(jnp.int32, main.shape, 0) == 0
    first_lane = lax.broadcasted_iota(jnp.int32, main.shape, 1) == 0
    lined = jnp.where(first_row, line, main)
    with_column = jnp.where(first_row, corner, column)
    kernels = (
        jnp.concatenate([main, jnp.where(first_lane, column, main)], 1),
        jnp.concatenate([lined, jnp.where(first_lane, with_column, lined)], 1),
    )
    p = split(dot3(split(r), (y_ref[0], y_ref[1]), NN))
    y_back = (y_back_ref[0], y_back_ref[1])
    u = []
    for part in range(2):
        at = slice(part * half, (part + 1) * half)
        q = dot3((x_ref[0, at], x_ref[1, at]), p, NN) * kernels[part]
        u.append(dot3(split(q), y_back, NN))
    v = dot3((x_back_ref[0], x_back_ref[1]), split(jnp.concatenate(u, 0)), NN)
    for h in range(blocks_b // per):
        lanes = slice(h * per * slab_y, (h + 1) * per * slab_y)
        v_h = exchange_blocks([v[n * blocks_a : (n + 1) * blocks_a, lanes] for n in range(per)], slab_y)
        for n in range(per):
            done = 0
            for start, step, count in runs[h * per + n]:
                out_ref[pl.ds(start, count, stride=step), :] = v_h[n][done : done + count]
                done += count


def inverse_z(r_ref, t_ref, out_ref):
    out = dot3(split(r_ref[...].T), (t_ref[0], t_ref[1]), NN)
    out_ref[...] = out.reshape(out_ref.shape)


def strided(values):
    runs, at = [], 0
    while at < len(values):
        step = values[at + 1] - values[at] if at + 1 < len(values) else 1
        count = 1
        while at + count < len(values) and values[at + count] - values[at + count - 1] == step:
            count += 1
        runs.append((int(values[at]), int(step), count))
        at += count
    return tuple(runs)


def call(kernel, shape, operands, flops):
    size = sum(x.size * x.dtype.itemsize for x in operands) + 4 * int(np.prod(shape))
    return pl.pallas_call(
        kernel,
        out_shape=jax.ShapeDtypeStruct(shape, jnp.float32),
        in_specs=[VMEM] * len(operands),
        out_specs=VMEM,
        compiler_params=pltpu.CompilerParams(vmem_limit_bytes=40 * 1024 * 1024),
        cost_estimate=pl.CostEstimate(flops=flops, bytes_accessed=size, transcendentals=0),
    )(*operands)


def body(density, kernel_hat):
    blocks_a = lax.axis_size(GA)
    blocks_b = lax.axis_size(COL)
    slab_x, slab_y, cells = density.shape
    length = 2 * cells
    per_b, per_c = kernel_hat.shape[:2]
    weights = np.full((2, cells), 2.0 / length)
    weights[:, 0] = 1.0 / length
    weights = weights.reshape(length, 1)

    sizes = {name: lax.axis_size(name) for name in RANKS}
    where = dict(zip(RANKS, np.indices(tuple(sizes.values())).reshape(len(RANKS), -1)))
    index_a = np.ravel_multi_index([where[n] for n in GA], [sizes[n] for n in GA])
    index_b = np.ravel_multi_index([where[n] for n in COL], [sizes[n] for n in COL])
    ranks = np.empty((blocks_a, blocks_b), np.int64)
    ranks[index_a, index_b] = np.arange(len(index_a))
    order_blocks = np.argsort(ranks[:, 0])
    runs = tuple(strided(ranks[order_blocks, n]) for n in range(blocks_b))

    modes_z = modes(np.arange(cells), cells - np.arange(cells), cells, length)
    tz = halves(modes_z)
    tz_back = halves((weights * modes_z)[per_c * index_b + index_a])
    sub, owner = np.divmod(np.arange(cells), blocks_a)
    order_b = np.where(owner < blocks_a // 2, per_b * owner + sub, length - 1 - per_b * owner - sub)
    modes_y = modes(order_b, np.where(order_b == 0, cells, order_b), cells, length)
    ty, ty_back = halves(modes_y.T), halves(weights * modes_y)
    order_a = np.arange(cells)
    modes_x = modes(order_a, np.where(order_a == 0, cells, order_a), cells, length)
    order_x = np.arange(cells).reshape(blocks_a, slab_x).T
    tx = halves(modes_x[:, order_x.reshape(-1)])
    tx_back = halves((weights * modes_x)[:, order_x[:, order_blocks].reshape(-1)].T)

    rows, tiles = cells // blocks_a, cells // 128
    total = blocks_b + (rows + 1) * tiles + 1
    places = dict(blocks_a=blocks_a, blocks_b=blocks_b, slab_x=slab_x, slab_y=slab_y)

    sent = pl.pallas_call(
        forward_z,
        out_shape=jax.ShapeDtypeStruct((length, slab_x * slab_y), jnp.float32),
        in_specs=[pl.BlockSpec(memory_space=pltpu.HBM)] * 2,
        out_specs=VMEM,
        scratch_shapes=[
            pltpu.VMEM(density.shape, jnp.float32),
            pltpu.VMEM(tz.shape, jnp.bfloat16),
            pltpu.SemaphoreType.DMA((2,)),
        ],
        compiler_params=pltpu.CompilerParams(vmem_limit_bytes=8 * 1024 * 1024),
        cost_estimate=pl.CostEstimate(flops=6 * 128 * 256 * 512, bytes_accessed=2**20, transcendentals=0),
    )(density, tz)
    got = lax.all_to_all(sent, COL, split_axis=0, concat_axis=0, tiled=True)
    packed = call(functools.partial(pack, **places), (blocks_a * total, 128), (got, kernel_hat), 0)
    got = lax.all_to_all(packed.reshape(blocks_a, 1, total * 128), GA, split_axis=0, concat_axis=0, tiled=True)
    back = call(
        functools.partial(convolve, runs=runs, **places),
        (length, slab_x * slab_y),
        (got.reshape(blocks_a * total, 128), ty, tx, ty_back, tx_back),
        6 * 200 * 10**6,
    )
    got = lax.all_to_all(back, RANKS, split_axis=0, concat_axis=0, tiled=True)
    return call(inverse_z, density.shape, (got, tz_back), 6 * 128 * 256 * 512)


def solution(mesh):
    devices = mesh.devices
    grp, row, col = devices.shape
    parts = Mesh(devices.reshape(grp, row // 2, 2, 2, col // 2), ("grp", "ra", "rb", "ca", "cb"))
    return jax.shard_map(
        body,
        mesh=parts,
        in_specs=(P(GA, COL, None), P(GA, COL, None)),
        out_specs=P(GA, COL, None),
        check_vma=False,
    )
```

```python
import functools
import math

import jax
import jax.numpy as jnp
import ml_dtypes
import numpy as np
from jax import lax
from jax.experimental import pallas as pl
from jax.experimental.pallas import tpu as pltpu
from jax.sharding import Mesh
from jax.sharding import PartitionSpec as P


GA = ("grp", "ra", "rb")
COL = ("ca", "cb")
RANKS = ("grp", "cb", "ra", "rb", "ca")
NN = (((1,), (0,)), ((), ()))
NT = (((1,), (1,)), ((), ()))
VMEM = pl.BlockSpec(memory_space=pltpu.VMEM)


def modes(freqs_c, freqs_s, cells, length):
    centre = np.arange(cells) - (cells - 1) / 2.0
    angle = 2.0 * np.pi / length
    return np.concatenate(
        [np.cos(angle * np.outer(freqs_c, centre)), np.sin(angle * np.outer(freqs_s, centre))], 0
    )


def halves(table):
    table = np.asarray(table, np.float32)
    hi = table.astype(ml_dtypes.bfloat16)
    lo = (table - hi.astype(np.float32)).astype(ml_dtypes.bfloat16)
    return jnp.asarray(np.stack([hi, lo]))


def split(x):
    hi = x.astype(jnp.bfloat16)
    return hi, (x - hi.astype(jnp.float32)).astype(jnp.bfloat16)


def dot3(left, right, dims):
    one = functools.partial(lax.dot_general, dimension_numbers=dims, preferred_element_type=jnp.float32)
    return one(left[0], right[0]) + (one(left[0], right[1]) + one(left[1], right[0]))


def exchange_blocks(v, block):
    count, lanes = len(v), v[0].shape[1]
    lane_block = lax.broadcasted_iota(jnp.int32, v[0].shape, 1) // block
    step = 1
    while step < count:
        odd = (lane_block & step) != 0
        w = list(v)
        for n in range(count):
            if n & step == 0:
                low, high = v[n], v[n + step]
                w[n] = jnp.where(odd, pltpu.roll(high, step * block, 1), low)
                w[n + step] = jnp.where(odd, high, pltpu.roll(low, lanes - step * block, 1))
        v = w
        step *= 2
    return v


def table_z(length, cells, step=16):
    def pair(rows, scale):
        n = lax.broadcasted_iota(jnp.int32, (rows, cells), 0) * scale
        offset = 2 * lax.broadcasted_iota(jnp.int32, (rows, cells), 1) - (cells - 1)
        turn = lax.rem(n * offset, 2 * length)
        angle = turn.astype(jnp.float32) * (math.pi / length)
        return jnp.cos(angle), jnp.sin(angle)

    cos_u, sin_u = pair(length // step, step)
    cos_v, sin_v = pair(step, 1)
    blocks = []
    for u in range(length // step):
        c, s = cos_u[u : u + 1], sin_u[u : u + 1]
        blocks.append(c * cos_v - s * sin_v if 2 * u * step < length else s * cos_v + c * sin_v)
    return jnp.concatenate(blocks, 0)


def forward_z(d_ref, out_ref):
    d = d_ref[...]
    d = d.reshape(d.shape[0] * d.shape[1], d.shape[2])
    out_ref[...] = dot3(split(table_z(out_ref.shape[0], d.shape[1])), split(d), NT)


def pack(r_ref, k_ref, out_ref, *, blocks_a, blocks_b, slab_x, slab_y):
    half = blocks_b * slab_y
    rows, tiles = half // blocks_a, half // 128
    total = out_ref.shape[0] // blocks_a

    def put(t, value):
        out_ref[pl.ds(t, blocks_a, stride=total), :] = value

    for h in range(blocks_b // slab_x):
        first = h * slab_x * blocks_a
        v = [r_ref[first + n * blocks_a : first + (n + 1) * blocks_a, :] for n in range(slab_x)]
        v = exchange_blocks(v, slab_y)
        for n in range(slab_x):
            put(h * slab_x + n, v[n])
    first = lax.axis_index("grp")
    lane = lax.broadcasted_iota(jnp.int32, (blocks_a, 128), 1)
    last = pltpu.roll(k_ref[0, :, half : half + 128], rows, 1)
    for s in range(rows):
        for h in range(tiles):
            put(blocks_b + s * tiles + h, k_ref[first + s, :, h * 128 : (h + 1) * 128])
        column = k_ref[first + s, :, half : half + 128]
        last = jnp.where(lane == s, pltpu.roll(column, s, 1) if s else column, last)
    for h in range(tiles):
        put(blocks_b + rows * tiles + h, k_ref[0, :, h * 128 : (h + 1) * 128])
    put(blocks_b + (rows + 1) * tiles, last)


def convolve(r_ref, y_ref, x_ref, y_back_ref, x_back_ref, out_ref, *, blocks_a, blocks_b, slab_x, slab_y, runs):
    half = blocks_b * slab_y
    rows, tiles = half // blocks_a, half // 128
    total = r_ref.shape[0] // blocks_a
    per = slab_x

    def take(t):
        return r_ref[pl.ds(t, blocks_a, stride=total), :]

    r = jnp.concatenate(
        [jnp.concatenate([take(h * per + n) for n in range(per)], 0) for h in range(blocks_b // per)], 1
    )
    main = jnp.concatenate(
        [
            jnp.concatenate([take(blocks_b + s * tiles + h) for s in range(rows)], 0).T
            for h in range(tiles)
        ],
        0,
    )
    tail = take(blocks_b + (rows + 1) * tiles).T
    line = jnp.concatenate([tail[s : s + 1] for s in range(rows)], 1)
    edge = blocks_a // 2 * total + blocks_b + rows * tiles
    column = jnp.concatenate(
        [jnp.broadcast_to(r_ref[edge + h : edge + h + 1, :], (8, 128)).T[:, :1] for h in range(tiles)], 0
    )
    corner = r_ref[edge + tiles : edge + tiles + 1, rows : rows + 1]
    first_row = lax.broadcasted_iota(jnp.int32, main.shape, 0) == 0
    first_lane = lax.broadcasted_iota(jnp.int32, main.shape, 1) == 0
    lined = jnp.where(first_row, line, main)
    with_column = jnp.where(first_row, corner, column)
    kernels = (
        jnp.concatenate([main, jnp.where(first_lane, column, main)], 1),
        jnp.concatenate([lined, jnp.where(first_lane, with_column, lined)], 1),
    )
    p = split(dot3(split(r), (y_ref[0], y_ref[1]), NN))
    y_back = (y_back_ref[0], y_back_ref[1])
    u = []
    for part in range(2):
        at = slice(part * half, (part + 1) * half)
        q = dot3((x_ref[0, at], x_ref[1, at]), p, NN) * kernels[part]
        u.append(dot3(split(q), y_back, NN))
    v = dot3((x_back_ref[0], x_back_ref[1]), split(jnp.concatenate(u, 0)), NN)
    for h in range(blocks_b // per):
        lanes = slice(h * per * slab_y, (h + 1) * per * slab_y)
        v_h = exchange_blocks([v[n * blocks_a : (n + 1) * blocks_a, lanes] for n in range(per)], slab_y)
        for n in range(per):
            done = 0
            for start, step, count in runs[h * per + n]:
                out_ref[pl.ds(start, count, stride=step), :] = v_h[n][done : done + count]
                done += count


def inverse_z(r_ref, t_ref, out_ref):
    out = dot3(split(r_ref[...].T), (t_ref[0], t_ref[1]), NN)
    out_ref[...] = out.reshape(out_ref.shape)


def strided(values):
    runs, at = [], 0
    while at < len(values):
        step = values[at + 1] - values[at] if at + 1 < len(values) else 1
        count = 1
        while at + count < len(values) and values[at + count] - values[at + count - 1] == step:
            count += 1
        runs.append((int(values[at]), int(step), count))
        at += count
    return tuple(runs)


def call(kernel, shape, operands, flops):
    size = sum(x.size * x.dtype.itemsize for x in operands) + 4 * int(np.prod(shape))
    return pl.pallas_call(
        kernel,
        out_shape=jax.ShapeDtypeStruct(shape, jnp.float32),
        in_specs=[VMEM] * len(operands),
        out_specs=VMEM,
        compiler_params=pltpu.CompilerParams(vmem_limit_bytes=40 * 1024 * 1024),
        cost_estimate=pl.CostEstimate(flops=flops, bytes_accessed=size, transcendentals=0),
    )(*operands)


def body(density, kernel_hat):
    blocks_a = lax.axis_size(GA)
    blocks_b = lax.axis_size(COL)
    slab_x, slab_y, cells = density.shape
    length = 2 * cells
    per_b, per_c = kernel_hat.shape[:2]
    weights = np.full((2, cells), 2.0 / length)
    weights[:, 0] = 1.0 / length
    weights = weights.reshape(length, 1)

    sizes = {name: lax.axis_size(name) for name in RANKS}
    where = dict(zip(RANKS, np.indices(tuple(sizes.values())).reshape(len(RANKS), -1)))
    index_a = np.ravel_multi_index([where[n] for n in GA], [sizes[n] for n in GA])
    index_b = np.ravel_multi_index([where[n] for n in COL], [sizes[n] for n in COL])
    ranks = np.empty((blocks_a, blocks_b), np.int64)
    ranks[index_a, index_b] = np.arange(len(index_a))
    order_blocks = np.argsort(ranks[:, 0])
    runs = tuple(strided(ranks[order_blocks, n]) for n in range(blocks_b))

    modes_z = modes(np.arange(cells), cells - np.arange(cells), cells, length)
    tz_back = halves((weights * modes_z)[per_c * index_b + index_a])
    sub, owner = np.divmod(np.arange(cells), blocks_a)
    order_b = np.where(owner < blocks_a // 2, per_b * owner + sub, length - 1 - per_b * owner - sub)
    modes_y = modes(order_b, np.where(order_b == 0, cells, order_b), cells, length)
    ty, ty_back = halves(modes_y.T), halves(weights * modes_y)
    order_a = np.arange(cells)
    modes_x = modes(order_a, np.where(order_a == 0, cells, order_a), cells, length)
    order_x = np.arange(cells).reshape(blocks_a, slab_x).T
    tx = halves(modes_x[:, order_x.reshape(-1)])
    tx_back = halves((weights * modes_x)[:, order_x[:, order_blocks].reshape(-1)].T)

    rows, tiles = cells // blocks_a, cells // 128
    total = blocks_b + (rows + 1) * tiles + 1
    places = dict(blocks_a=blocks_a, blocks_b=blocks_b, slab_x=slab_x, slab_y=slab_y)

    sent = call(forward_z, (length, slab_x * slab_y), (density,), 10**9)
    got = lax.all_to_all(sent, COL, split_axis=0, concat_axis=0, tiled=True)
    packed = call(functools.partial(pack, **places), (blocks_a * total, 128), (got, kernel_hat), 0)
    got = lax.all_to_all(packed.reshape(blocks_a, 1, total * 128), GA, split_axis=0, concat_axis=0, tiled=True)
    back = call(
        functools.partial(convolve, runs=runs, **places),
        (length, slab_x * slab_y),
        (got.reshape(blocks_a * total, 128), ty, tx, ty_back, tx_back),
        6 * 200 * 10**6,
    )
    got = lax.all_to_all(back, RANKS, split_axis=0, concat_axis=0, tiled=True)
    return call(inverse_z, density.shape, (got, tz_back), 6 * 128 * 256 * 512)


def solution(mesh):
    devices = mesh.devices
    grp, row, col = devices.shape
    parts = Mesh(devices.reshape(grp, row // 2, 2, 2, col // 2), ("grp", "ra", "rb", "ca", "cb"))
    return jax.shard_map(
        body,
        mesh=parts,
        in_specs=(P(GA, COL, None), P(GA, COL, None)),
        out_specs=P(GA, COL, None),
        check_vma=False,
    )
```

```python
import functools
import math

import jax
import jax.numpy as jnp
import ml_dtypes
import numpy as np
from jax import lax
from jax.experimental import pallas as pl
from jax.experimental.pallas import tpu as pltpu
from jax.sharding import Mesh
from jax.sharding import PartitionSpec as P


GA = ("grp", "ra", "rb")
COL = ("ca", "cb")
RANKS = ("grp", "cb", "ra", "rb", "ca")
NN = (((1,), (0,)), ((), ()))
NT = (((1,), (1,)), ((), ()))
VMEM = pl.BlockSpec(memory_space=pltpu.VMEM)


def modes(freqs_c, freqs_s, cells, length):
    centre = np.arange(cells) - (cells - 1) / 2.0
    angle = 2.0 * np.pi / length
    return np.concatenate(
        [np.cos(angle * np.outer(freqs_c, centre)), np.sin(angle * np.outer(freqs_s, centre))], 0
    )


def halves(table):
    table = np.asarray(table, np.float32)
    hi = table.astype(ml_dtypes.bfloat16)
    lo = (table - hi.astype(np.float32)).astype(ml_dtypes.bfloat16)
    return jnp.asarray(np.stack([hi, lo]))


def split(x):
    hi = x.astype(jnp.bfloat16)
    return hi, (x - hi.astype(jnp.float32)).astype(jnp.bfloat16)


def dot3(left, right, dims):
    one = functools.partial(lax.dot_general, dimension_numbers=dims, preferred_element_type=jnp.float32)
    return one(left[0], right[0]) + (one(left[0], right[1]) + one(left[1], right[0]))


def exchange_blocks(v, block):
    count, lanes = len(v), v[0].shape[1]
    lane_block = lax.broadcasted_iota(jnp.int32, v[0].shape, 1) // block
    step = 1
    while step < count:
        odd = (lane_block & step) != 0
        w = list(v)
        for n in range(count):
            if n & step == 0:
                low, high = v[n], v[n + step]
                w[n] = jnp.where(odd, pltpu.roll(high, step * block, 1), low)
                w[n + step] = jnp.where(odd, high, pltpu.roll(low, lanes - step * block, 1))
        v = w
        step *= 2
    return v


def table_z(length, cells, step=16):
    def pair(rows, scale):
        n = lax.broadcasted_iota(jnp.int32, (rows, cells), 0) * scale
        offset = 2 * lax.broadcasted_iota(jnp.int32, (rows, cells), 1) - (cells - 1)
        turn = lax.rem(n * offset, 2 * length)
        angle = turn.astype(jnp.float32) * (math.pi / length)
        return jnp.cos(angle), jnp.sin(angle)

    cos_u, sin_u = pair(length // step, step)
    cos_v, sin_v = pair(step, 1)
    blocks = []
    for u in range(length // step):
        c, s = cos_u[u : u + 1], sin_u[u : u + 1]
        blocks.append(c * cos_v - s * sin_v if 2 * u * step < length else s * cos_v + c * sin_v)
    return jnp.concatenate(blocks, 0)


def forward_z(d_ref, out_ref):
    d = d_ref[...]
    d = d.reshape(d.shape[0] * d.shape[1], d.shape[2])
    out_ref[...] = dot3(split(table_z(out_ref.shape[0], d.shape[1])), split(d), NT)


def pack(r_ref, k_ref, out_ref, *, blocks_a, blocks_b, slab_x, slab_y):
    half = blocks_b * slab_y
    rows, tiles = half // blocks_a, half // 128
    total = out_ref.shape[0] // blocks_a

    def put(t, value):
        out_ref[pl.ds(t, blocks_a, stride=total), :] = value

    for h in range(blocks_b // slab_x):
        first = h * slab_x * blocks_a
        v = [r_ref[first + n * blocks_a : first + (n + 1) * blocks_a, :] for n in range(slab_x)]
        v = exchange_blocks(v, slab_y)
        for n in range(slab_x):
            put(h * slab_x + n, v[n])
    first = lax.axis_index("grp")
    edge = jnp.logical_and(first == 1, lax.axis_index("ra") + lax.axis_index("rb") == 0)
    lane = lax.broadcasted_iota(jnp.int32, (blocks_a, 128), 1)
    last = pltpu.roll(k_ref[0, :, half : half + 128], rows, 1)
    end = half - 128
    for s in range(rows):
        for h in range(tiles):
            tile = k_ref[first + s, :, h * 128 : (h + 1) * 128]
            if s == rows - 1 and h == tiles - 1:
                tile = jnp.where(edge, k_ref[0, :, end:half], tile)
            put(blocks_b + s * tiles + h, tile)
        column = k_ref[first + s, :, half : half + 128]
        last = jnp.where(lane == s, pltpu.roll(column, s, 1) if s else column, last)
    put(blocks_b + rows * tiles, jnp.where(edge, k_ref[0, :, :128], k_ref[rows, :, end:half]))
    put(blocks_b + rows * tiles + 1, last)


def convolve(r_ref, y_ref, x_ref, y_back_ref, x_back_ref, out_ref, *, blocks_a, blocks_b, slab_x, slab_y, runs):
    half = blocks_b * slab_y
    rows, tiles = half // blocks_a, half // 128
    total = r_ref.shape[0] // blocks_a
    per = slab_x

    def take(t):
        return r_ref[pl.ds(t, blocks_a, stride=total), :]

    r = jnp.concatenate(
        [jnp.concatenate([take(h * per + n) for n in range(per)], 0) for h in range(blocks_b // per)], 1
    )
    spare, middle = blocks_b + rows * tiles, blocks_a // 2

    def kernel_tile(s, h):
        tile = take(blocks_b + s * tiles + h)
        if s == rows - 1 and h == tiles - 1:
            at = (middle - 1) * total + spare
            owner = lax.broadcasted_iota(jnp.int32, tile.shape, 0)
            tile = jnp.where(owner == middle, r_ref[at : at + 1, :], tile)
        return tile

    main = jnp.concatenate(
        [jnp.concatenate([kernel_tile(s, h) for s in range(rows)], 0).T for h in range(tiles)], 0
    )
    tail = take(spare + 1).T
    line = jnp.concatenate([tail[s : s + 1] for s in range(rows)], 1)
    at = middle * total + spare
    column = jnp.concatenate(
        [jnp.broadcast_to(r_ref[n : n + 1, :], (8, 128)).T[:, :1] for n in (at, at - 1)], 0
    )
    corner = r_ref[at + 1 : at + 2, rows : rows + 1]
    first_row = lax.broadcasted_iota(jnp.int32, main.shape, 0) == 0
    first_lane = lax.broadcasted_iota(jnp.int32, main.shape, 1) == 0
    lined = jnp.where(first_row, line, main)
    with_column = jnp.where(first_row, corner, column)
    kernels = (
        jnp.concatenate([main, jnp.where(first_lane, column, main)], 1),
        jnp.concatenate([lined, jnp.where(first_lane, with_column, lined)], 1),
    )
    p = split(dot3(split(r), (y_ref[0], y_ref[1]), NN))
    y_back = (y_back_ref[0], y_back_ref[1])
    u = []
    for part in range(2):
        at = slice(part * half, (part + 1) * half)
        q = dot3((x_ref[0, at], x_ref[1, at]), p, NN) * kernels[part]
        u.append(dot3(split(q), y_back, NN))
    v = dot3((x_back_ref[0], x_back_ref[1]), split(jnp.concatenate(u, 0)), NN)
    for h in range(blocks_b // per):
        lanes = slice(h * per * slab_y, (h + 1) * per * slab_y)
        v_h = exchange_blocks([v[n * blocks_a : (n + 1) * blocks_a, lanes] for n in range(per)], slab_y)
        for n in range(per):
            done = 0
            for start, step, count in runs[h * per + n]:
                out_ref[pl.ds(start, count, stride=step), :] = v_h[n][done : done + count]
                done += count


def inverse_z(r_ref, t_ref, out_ref):
    out = dot3(split(r_ref[...].T), (t_ref[0], t_ref[1]), NN)
    out_ref[...] = out.reshape(out_ref.shape)


def strided(values):
    runs, at = [], 0
    while at < len(values):
        step = values[at + 1] - values[at] if at + 1 < len(values) else 1
        count = 1
        while at + count < len(values) and values[at + count] - values[at + count - 1] == step:
            count += 1
        runs.append((int(values[at]), int(step), count))
        at += count
    return tuple(runs)


def call(kernel, shape, operands, flops):
    size = sum(x.size * x.dtype.itemsize for x in operands) + 4 * int(np.prod(shape))
    return pl.pallas_call(
        kernel,
        out_shape=jax.ShapeDtypeStruct(shape, jnp.float32),
        in_specs=[VMEM] * len(operands),
        out_specs=VMEM,
        compiler_params=pltpu.CompilerParams(vmem_limit_bytes=40 * 1024 * 1024),
        cost_estimate=pl.CostEstimate(flops=flops, bytes_accessed=size, transcendentals=0),
    )(*operands)


def body(density, kernel_hat):
    blocks_a = lax.axis_size(GA)
    blocks_b = lax.axis_size(COL)
    slab_x, slab_y, cells = density.shape
    length = 2 * cells
    per_b, per_c = kernel_hat.shape[:2]
    weights = np.full((2, cells), 2.0 / length)
    weights[:, 0] = 1.0 / length
    weights = weights.reshape(length, 1)

    sizes = {name: lax.axis_size(name) for name in RANKS}
    where = dict(zip(RANKS, np.indices(tuple(sizes.values())).reshape(len(RANKS), -1)))
    index_a = np.ravel_multi_index([where[n] for n in GA], [sizes[n] for n in GA])
    index_b = np.ravel_multi_index([where[n] for n in COL], [sizes[n] for n in COL])
    ranks = np.empty((blocks_a, blocks_b), np.int64)
    ranks[index_a, index_b] = np.arange(len(index_a))
    order_blocks = np.argsort(ranks[:, 0])
    runs = tuple(strided(ranks[order_blocks, n]) for n in range(blocks_b))

    modes_z = modes(np.arange(cells), cells - np.arange(cells), cells, length)
    tz_back = halves((weights * modes_z)[per_c * index_b + index_a])
    sub, owner = np.divmod(np.arange(cells), blocks_a)
    order_b = np.where(owner < blocks_a // 2, per_b * owner + sub, length - 1 - per_b * owner - sub)
    modes_y = modes(order_b, np.where(order_b == 0, cells, order_b), cells, length)
    ty, ty_back = halves(modes_y.T), halves(weights * modes_y)
    order_a = np.arange(cells)
    modes_x = modes(order_a, np.where(order_a == 0, cells, order_a), cells, length)
    order_x = np.arange(cells).reshape(blocks_a, slab_x).T
    tx = halves(modes_x[:, order_x.reshape(-1)])
    tx_back = halves((weights * modes_x)[:, order_x[:, order_blocks].reshape(-1)].T)

    rows, tiles = cells // blocks_a, cells // 128
    total = blocks_b + rows * tiles + 2
    places = dict(blocks_a=blocks_a, blocks_b=blocks_b, slab_x=slab_x, slab_y=slab_y)

    sent = call(forward_z, (length, slab_x * slab_y), (density,), 10**9)
    got = lax.all_to_all(sent, COL, split_axis=0, concat_axis=0, tiled=True)
    packed = call(functools.partial(pack, **places), (blocks_a * total, 128), (got, kernel_hat), 0)
    got = lax.all_to_all(packed.reshape(blocks_a, 1, total * 128), GA, split_axis=0, concat_axis=0, tiled=True)
    back = call(
        functools.partial(convolve, runs=runs, **places),
        (length, slab_x * slab_y),
        (got.reshape(blocks_a * total, 128), ty, tx, ty_back, tx_back),
        6 * 200 * 10**6,
    )
    got = lax.all_to_all(back, RANKS, split_axis=0, concat_axis=0, tiled=True)
    return call(inverse_z, density.shape, (got, tz_back), 6 * 128 * 256 * 512)


def solution(mesh):
    devices = mesh.devices
    grp, row, col = devices.shape
    parts = Mesh(devices.reshape(grp, row // 2, 2, 2, col // 2), ("grp", "ra", "rb", "ca", "cb"))
    return jax.shard_map(
        body,
        mesh=parts,
        in_specs=(P(GA, COL, None), P(GA, COL, None)),
        out_specs=P(GA, COL, None),
        check_vma=False,
    )
```

```python
import functools
import math

import jax
import jax.numpy as jnp
import ml_dtypes
import numpy as np
from jax import lax
from jax.experimental import pallas as pl
from jax.experimental.pallas import tpu as pltpu
from jax.sharding import Mesh
from jax.sharding import PartitionSpec as P


GA = ("grp", "ra", "rb")
COL = ("ca", "cb")
RANKS = ("grp", "ra", "cb", "ca", "rb")
NN = (((1,), (0,)), ((), ()))
NT = (((1,), (1,)), ((), ()))
VMEM = pl.BlockSpec(memory_space=pltpu.VMEM)


def modes(freqs_c, freqs_s, cells, length):
    centre = np.arange(cells) - (cells - 1) / 2.0
    angle = 2.0 * np.pi / length
    return np.concatenate(
        [np.cos(angle * np.outer(freqs_c, centre)), np.sin(angle * np.outer(freqs_s, centre))], 0
    )


def halves(table):
    table = np.asarray(table, np.float32)
    hi = table.astype(ml_dtypes.bfloat16)
    lo = (table - hi.astype(np.float32)).astype(ml_dtypes.bfloat16)
    return jnp.asarray(np.stack([hi, lo]))


def split(x):
    hi = x.astype(jnp.bfloat16)
    return hi, (x - hi.astype(jnp.float32)).astype(jnp.bfloat16)


def dot3(left, right, dims):
    one = functools.partial(lax.dot_general, dimension_numbers=dims, preferred_element_type=jnp.float32)
    return one(left[0], right[0]) + (one(left[0], right[1]) + one(left[1], right[0]))


def exchange_blocks(v, block):
    count, lanes = len(v), v[0].shape[1]
    lane_block = lax.broadcasted_iota(jnp.int32, v[0].shape, 1) // block
    step = 1
    while step < count:
        odd = (lane_block & step) != 0
        w = list(v)
        for n in range(count):
            if n & step == 0:
                low, high = v[n], v[n + step]
                w[n] = jnp.where(odd, pltpu.roll(high, step * block, 1), low)
                w[n + step] = jnp.where(odd, high, pltpu.roll(low, lanes - step * block, 1))
        v = w
        step *= 2
    return v


def table_z(length, cells, step=16):
    def pair(rows, scale):
        n = lax.broadcasted_iota(jnp.int32, (rows, cells), 0) * scale
        offset = 2 * lax.broadcasted_iota(jnp.int32, (rows, cells), 1) - (cells - 1)
        turn = lax.rem(n * offset, 2 * length)
        angle = turn.astype(jnp.float32) * (math.pi / length)
        return jnp.cos(angle), jnp.sin(angle)

    cos_u, sin_u = pair(length // step, step)
    cos_v, sin_v = pair(step, 1)
    blocks = []
    for u in range(length // step):
        c, s = cos_u[u : u + 1], sin_u[u : u + 1]
        blocks.append(c * cos_v - s * sin_v if 2 * u * step < length else s * cos_v + c * sin_v)
    return jnp.concatenate(blocks, 0)


def forward_z(d_ref, out_ref):
    d = d_ref[...]
    d = d.reshape(d.shape[0] * d.shape[1], d.shape[2])
    out_ref[...] = dot3(split(table_z(out_ref.shape[0], d.shape[1])), split(d), NT)


def pack(r_ref, k_ref, out_ref, *, blocks_a, blocks_b, slab_x, slab_y):
    half = blocks_b * slab_y
    rows, tiles = half // blocks_a, half // 128
    total = out_ref.shape[0] // blocks_a

    def put(t, value):
        out_ref[pl.ds(t, blocks_a, stride=total), :] = value

    for h in range(blocks_b // slab_x):
        first = h * slab_x * blocks_a
        v = [r_ref[first + n * blocks_a : first + (n + 1) * blocks_a, :] for n in range(slab_x)]
        v = exchange_blocks(v, slab_y)
        for n in range(slab_x):
            put(h * slab_x + n, v[n])
    first = lax.axis_index("grp")
    edge = jnp.logical_and(first == 1, lax.axis_index("ra") + lax.axis_index("rb") == 0)
    lane = lax.broadcasted_iota(jnp.int32, (blocks_a, 128), 1)
    last = pltpu.roll(k_ref[0, :, half : half + 128], rows, 1)
    end = half - 128
    for s in range(rows):
        for h in range(tiles):
            tile = k_ref[first + s, :, h * 128 : (h + 1) * 128]
            if s == rows - 1 and h == tiles - 1:
                tile = jnp.where(edge, k_ref[0, :, end:half], tile)
            put(blocks_b + s * tiles + h, tile)
        column = k_ref[first + s, :, half : half + 128]
        last = jnp.where(lane == s, pltpu.roll(column, s, 1) if s else column, last)
    put(blocks_b + rows * tiles, jnp.where(edge, k_ref[0, :, :128], k_ref[rows, :, end:half]))
    put(blocks_b + rows * tiles + 1, last)


def convolve(r_ref, y_ref, x_ref, y_back_ref, x_back_ref, out_ref, *, blocks_a, blocks_b, slab_x, slab_y, runs):
    half = blocks_b * slab_y
    rows, tiles = half // blocks_a, half // 128
    total = r_ref.shape[0] // blocks_a
    per = slab_x

    def take(t):
        return r_ref[pl.ds(t, blocks_a, stride=total), :]

    r = jnp.concatenate(
        [jnp.concatenate([take(h * per + n) for n in range(per)], 0) for h in range(blocks_b // per)], 1
    )
    spare, middle = blocks_b + rows * tiles, blocks_a // 2

    def kernel_tile(s, h):
        tile = take(blocks_b + s * tiles + h)
        if s == rows - 1 and h == tiles - 1:
            at = (middle - 1) * total + spare
            owner = lax.broadcasted_iota(jnp.int32, tile.shape, 0)
            tile = jnp.where(owner == middle, r_ref[at : at + 1, :], tile)
        return tile

    main = jnp.concatenate(
        [jnp.concatenate([kernel_tile(s, h) for s in range(rows)], 0).T for h in range(tiles)], 0
    )
    tail = take(spare + 1).T
    line = jnp.concatenate([tail[s : s + 1] for s in range(rows)], 1)
    at = middle * total + spare
    column = jnp.concatenate(
        [jnp.broadcast_to(r_ref[n : n + 1, :], (8, 128)).T[:, :1] for n in (at, at - 1)], 0
    )
    corner = r_ref[at + 1 : at + 2, rows : rows + 1]
    first_row = lax.broadcasted_iota(jnp.int32, main.shape, 0) == 0
    first_lane = lax.broadcasted_iota(jnp.int32, main.shape, 1) == 0
    lined = jnp.where(first_row, line, main)
    with_column = jnp.where(first_row, corner, column)
    kernels = (
        jnp.concatenate([main, jnp.where(first_lane, column, main)], 1),
        jnp.concatenate([lined, jnp.where(first_lane, with_column, lined)], 1),
    )
    p = split(dot3(split(r), (y_ref[0], y_ref[1]), NN))
    y_back = (y_back_ref[0], y_back_ref[1])
    u = []
    for part in range(2):
        at = slice(part * half, (part + 1) * half)
        q = dot3((x_ref[0, at], x_ref[1, at]), p, NN) * kernels[part]
        u.append(dot3(split(q), y_back, NN))
    v = dot3((x_back_ref[0], x_back_ref[1]), split(jnp.concatenate(u, 0)), NN)
    for h in range(blocks_b // per):
        lanes = slice(h * per * slab_y, (h + 1) * per * slab_y)
        v_h = exchange_blocks([v[n * blocks_a : (n + 1) * blocks_a, lanes] for n in range(per)], slab_y)
        for n in range(per):
            done = 0
            for start, step, count in runs[h * per + n]:
                out_ref[pl.ds(start, count, stride=step), :] = v_h[n][done : done + count]
                done += count


def inverse_z(r_ref, t_ref, out_ref):
    out = dot3(split(r_ref[...].T), (t_ref[0], t_ref[1]), NN)
    out_ref[...] = out.reshape(out_ref.shape)


def strided(values):
    runs, at = [], 0
    while at < len(values):
        step = values[at + 1] - values[at] if at + 1 < len(values) else 1
        count = 1
        while at + count < len(values) and values[at + count] - values[at + count - 1] == step:
            count += 1
        runs.append((int(values[at]), int(step), count))
        at += count
    return tuple(runs)


def call(kernel, shape, operands, flops):
    size = sum(x.size * x.dtype.itemsize for x in operands) + 4 * int(np.prod(shape))
    return pl.pallas_call(
        kernel,
        out_shape=jax.ShapeDtypeStruct(shape, jnp.float32),
        in_specs=[VMEM] * len(operands),
        out_specs=VMEM,
        compiler_params=pltpu.CompilerParams(vmem_limit_bytes=40 * 1024 * 1024),
        cost_estimate=pl.CostEstimate(flops=flops, bytes_accessed=size, transcendentals=0),
    )(*operands)


def body(density, kernel_hat):
    blocks_a = lax.axis_size(GA)
    blocks_b = lax.axis_size(COL)
    slab_x, slab_y, cells = density.shape
    length = 2 * cells
    per_b, per_c = kernel_hat.shape[:2]
    weights = np.full((2, cells), 2.0 / length)
    weights[:, 0] = 1.0 / length
    weights = weights.reshape(length, 1)

    sizes = {name: lax.axis_size(name) for name in RANKS}
    where = dict(zip(RANKS, np.indices(tuple(sizes.values())).reshape(len(RANKS), -1)))
    index_a = np.ravel_multi_index([where[n] for n in GA], [sizes[n] for n in GA])
    index_b = np.ravel_multi_index([where[n] for n in COL], [sizes[n] for n in COL])
    ranks = np.empty((blocks_a, blocks_b), np.int64)
    ranks[index_a, index_b] = np.arange(len(index_a))
    order_blocks = np.argsort(ranks[:, 0])
    runs = tuple(strided(ranks[order_blocks, n]) for n in range(blocks_b))

    modes_z = modes(np.arange(cells), cells - np.arange(cells), cells, length)
    tz_back = halves((weights * modes_z)[per_c * index_b + index_a])
    sub, owner = np.divmod(np.arange(cells), blocks_a)
    order_b = np.where(owner < blocks_a // 2, per_b * owner + sub, length - 1 - per_b * owner - sub)
    modes_y = modes(order_b, np.where(order_b == 0, cells, order_b), cells, length)
    ty, ty_back = halves(modes_y.T), halves(weights * modes_y)
    order_a = np.arange(cells)
    modes_x = modes(order_a, np.where(order_a == 0, cells, order_a), cells, length)
    order_x = np.arange(cells).reshape(blocks_a, slab_x).T
    tx = halves(modes_x[:, order_x.reshape(-1)])
    tx_back = halves((weights * modes_x)[:, order_x[:, order_blocks].reshape(-1)].T)

    rows, tiles = cells // blocks_a, cells // 128
    total = blocks_b + rows * tiles + 2
    places = dict(blocks_a=blocks_a, blocks_b=blocks_b, slab_x=slab_x, slab_y=slab_y)

    sent = call(forward_z, (length, slab_x * slab_y), (density,), 10**9)
    got = lax.all_to_all(sent, COL, split_axis=0, concat_axis=0, tiled=True)
    packed = call(functools.partial(pack, **places), (blocks_a * total, 128), (got, kernel_hat), 0)
    got = lax.all_to_all(packed.reshape(blocks_a, 1, total * 128), GA, split_axis=0, concat_axis=0, tiled=True)
    back = call(
        functools.partial(convolve, runs=runs, **places),
        (length, slab_x * slab_y),
        (got.reshape(blocks_a * total, 128), ty, tx, ty_back, tx_back),
        6 * 200 * 10**6,
    )
    got = lax.all_to_all(back, RANKS, split_axis=0, concat_axis=0, tiled=True)
    return call(inverse_z, density.shape, (got, tz_back), 6 * 128 * 256 * 512)


def solution(mesh):
    devices = mesh.devices
    grp, row, col = devices.shape
    parts = Mesh(devices.reshape(grp, row // 2, 2, 2, col // 2), ("grp", "ra", "rb", "ca", "cb"))
    return jax.shard_map(
        body,
        mesh=parts,
        in_specs=(P(GA, COL, None), P(GA, COL, None)),
        out_specs=P(GA, COL, None),
        check_vma=False,
    )
```

```python
import functools
import math

import jax
import jax.numpy as jnp
import ml_dtypes
import numpy as np
from jax import lax
from jax.experimental import pallas as pl
from jax.experimental.pallas import tpu as pltpu
from jax.sharding import Mesh
from jax.sharding import PartitionSpec as P


GA = ("grp", "ra", "rb")
COL = ("ca", "cb")
RANKS = ("grp", "ra", "cb", "ca", "rb")
NN = (((1,), (0,)), ((), ()))
NT = (((1,), (1,)), ((), ()))
VMEM = pl.BlockSpec(memory_space=pltpu.VMEM)


def modes(freqs_c, freqs_s, cells, length):
    centre = np.arange(cells) - (cells - 1) / 2.0
    angle = 2.0 * np.pi / length
    return np.concatenate(
        [np.cos(angle * np.outer(freqs_c, centre)), np.sin(angle * np.outer(freqs_s, centre))], 0
    )


def halves(table):
    table = np.asarray(table, np.float32)
    hi = table.astype(ml_dtypes.bfloat16)
    lo = (table - hi.astype(np.float32)).astype(ml_dtypes.bfloat16)
    return jnp.asarray(np.stack([hi, lo]))


def split(x):
    hi = x.astype(jnp.bfloat16)
    return hi, (x - hi.astype(jnp.float32)).astype(jnp.bfloat16)


def dot3(left, right, dims):
    one = functools.partial(lax.dot_general, dimension_numbers=dims, preferred_element_type=jnp.float32)
    return one(left[0], right[0]) + (one(left[0], right[1]) + one(left[1], right[0]))


def exchange_blocks(v, block):
    count, lanes = len(v), v[0].shape[1]
    lane_block = lax.broadcasted_iota(jnp.int32, v[0].shape, 1) // block
    step = 1
    while step < count:
        odd = (lane_block & step) != 0
        w = list(v)
        for n in range(count):
            if n & step == 0:
                low, high = v[n], v[n + step]
                w[n] = jnp.where(odd, pltpu.roll(high, step * block, 1), low)
                w[n + step] = jnp.where(odd, high, pltpu.roll(low, lanes - step * block, 1))
        v = w
        step *= 2
    return v


def table_z(length, cells, step=16):
    def pair(rows, scale):
        n = lax.broadcasted_iota(jnp.int32, (rows, cells), 0) * scale
        offset = 2 * lax.broadcasted_iota(jnp.int32, (rows, cells), 1) - (cells - 1)
        turn = lax.rem(n * offset, 2 * length)
        angle = turn.astype(jnp.float32) * (math.pi / length)
        return jnp.cos(angle), jnp.sin(angle)

    cos_u, sin_u = pair(length // step, step)
    cos_v, sin_v = pair(step, 1)
    blocks = []
    for u in range(length // step):
        c, s = cos_u[u : u + 1], sin_u[u : u + 1]
        blocks.append(c * cos_v - s * sin_v if 2 * u * step < length else s * cos_v + c * sin_v)
    return jnp.concatenate(blocks, 0)


def forward_z(d_ref, out_ref):
    d = d_ref[...]
    d = d.reshape(d.shape[0] * d.shape[1], d.shape[2])
    out_ref[...] = dot3(split(table_z(out_ref.shape[0], d.shape[1])), split(d), NT)


def pack(r_ref, k_ref, out_ref, *, blocks_a, blocks_b, slab_x, slab_y):
    half = blocks_b * slab_y
    rows, tiles = half // blocks_a, half // 128
    total = out_ref.shape[0] // blocks_a

    def put(t, value):
        out_ref[pl.ds(t, blocks_a, stride=total), :] = value

    for h in range(blocks_b // slab_x):
        first = h * slab_x * blocks_a
        v = [r_ref[first + n * blocks_a : first + (n + 1) * blocks_a, :] for n in range(slab_x)]
        v = exchange_blocks(v, slab_y)
        for n in range(slab_x):
            put(h * slab_x + n, v[n])
    first = lax.axis_index("grp")
    edge = jnp.logical_and(first == 1, lax.axis_index("ra") + lax.axis_index("rb") == 0)
    lane = lax.broadcasted_iota(jnp.int32, (blocks_a, 128), 1)
    last = pltpu.roll(k_ref[0, :, half : half + 128], rows, 1)
    end = half - 128
    for s in range(rows):
        for h in range(tiles):
            tile = k_ref[first + s, :, h * 128 : (h + 1) * 128]
            if s == rows - 1 and h == tiles - 1:
                tile = jnp.where(edge, k_ref[0, :, end:half], tile)
            put(blocks_b + s * tiles + h, tile)
        column = k_ref[first + s, :, half : half + 128]
        last = jnp.where(lane == s, pltpu.roll(column, s, 1) if s else column, last)
    put(blocks_b + rows * tiles, jnp.where(edge, k_ref[0, :, :128], k_ref[rows, :, end:half]))
    put(blocks_b + rows * tiles + 1, last)


def convolve(r_ref, y_ref, x_ref, y_back_ref, x_back_ref, out_ref, *, blocks_a, blocks_b, slab_x, slab_y, runs):
    half = blocks_b * slab_y
    rows, tiles = half // blocks_a, half // 128
    total = r_ref.shape[0] // blocks_a
    per = slab_x

    def take(t):
        return r_ref[pl.ds(t, blocks_a, stride=total), :]

    r = jnp.concatenate(
        [jnp.concatenate([take(h * per + n) for n in range(per)], 0) for h in range(blocks_b // per)], 1
    )
    p = split(dot3(split(r), (y_ref[0], y_ref[1]), NN))
    q0 = [dot3((x_ref[0, at], x_ref[1, at]), p, NN) for at in (slice(0, half), slice(half, 2 * half))]
    spare, middle = blocks_b + rows * tiles, blocks_a // 2

    def kernel_tile(s, h):
        tile = take(blocks_b + s * tiles + h)
        if s == rows - 1 and h == tiles - 1:
            at = (middle - 1) * total + spare
            owner = lax.broadcasted_iota(jnp.int32, tile.shape, 0)
            tile = jnp.where(owner == middle, r_ref[at : at + 1, :], tile)
        return tile

    main = jnp.concatenate(
        [jnp.concatenate([kernel_tile(s, h) for s in range(rows)], 0).T for h in range(tiles)], 0
    )
    tail = take(spare + 1).T
    line = jnp.concatenate([tail[s : s + 1] for s in range(rows)], 1)
    at = middle * total + spare
    column = jnp.concatenate(
        [jnp.broadcast_to(r_ref[n : n + 1, :], (8, 128)).T[:, :1] for n in (at, at - 1)], 0
    )
    corner = r_ref[at + 1 : at + 2, rows : rows + 1]
    first_row = lax.broadcasted_iota(jnp.int32, main.shape, 0) == 0
    first_lane = lax.broadcasted_iota(jnp.int32, main.shape, 1) == 0
    lined = jnp.where(first_row, line, main)
    with_column = jnp.where(first_row, corner, column)
    kernels = (
        jnp.concatenate([main, jnp.where(first_lane, column, main)], 1),
        jnp.concatenate([lined, jnp.where(first_lane, with_column, lined)], 1),
    )
    y_back = (y_back_ref[0], y_back_ref[1])
    u = []
    for part in range(2):
        u.append(dot3(split(q0[part] * kernels[part]), y_back, NN))
    v = dot3((x_back_ref[0], x_back_ref[1]), split(jnp.concatenate(u, 0)), NN)
    for h in range(blocks_b // per):
        lanes = slice(h * per * slab_y, (h + 1) * per * slab_y)
        v_h = exchange_blocks([v[n * blocks_a : (n + 1) * blocks_a, lanes] for n in range(per)], slab_y)
        for n in range(per):
            done = 0
            for start, step, count in runs[h * per + n]:
                out_ref[pl.ds(start, count, stride=step), :] = v_h[n][done : done + count]
                done += count


def inverse_z(r_ref, t_ref, out_ref):
    out = dot3(split(r_ref[...].T), (t_ref[0], t_ref[1]), NN)
    out_ref[...] = out.reshape(out_ref.shape)


def strided(values):
    runs, at = [], 0
    while at < len(values):
        step = values[at + 1] - values[at] if at + 1 < len(values) else 1
        count = 1
        while at + count < len(values) and values[at + count] - values[at + count - 1] == step:
            count += 1
        runs.append((int(values[at]), int(step), count))
        at += count
    return tuple(runs)


def call(kernel, shape, operands, flops):
    size = sum(x.size * x.dtype.itemsize for x in operands) + 4 * int(np.prod(shape))
    return pl.pallas_call(
        kernel,
        out_shape=jax.ShapeDtypeStruct(shape, jnp.float32),
        in_specs=[VMEM] * len(operands),
        out_specs=VMEM,
        compiler_params=pltpu.CompilerParams(vmem_limit_bytes=40 * 1024 * 1024),
        cost_estimate=pl.CostEstimate(flops=flops, bytes_accessed=size, transcendentals=0),
    )(*operands)


def body(density, kernel_hat):
    blocks_a = lax.axis_size(GA)
    blocks_b = lax.axis_size(COL)
    slab_x, slab_y, cells = density.shape
    length = 2 * cells
    per_b, per_c = kernel_hat.shape[:2]
    weights = np.full((2, cells), 2.0 / length)
    weights[:, 0] = 1.0 / length
    weights = weights.reshape(length, 1)

    sizes = {name: lax.axis_size(name) for name in RANKS}
    where = dict(zip(RANKS, np.indices(tuple(sizes.values())).reshape(len(RANKS), -1)))
    index_a = np.ravel_multi_index([where[n] for n in GA], [sizes[n] for n in GA])
    index_b = np.ravel_multi_index([where[n] for n in COL], [sizes[n] for n in COL])
    ranks = np.empty((blocks_a, blocks_b), np.int64)
    ranks[index_a, index_b] = np.arange(len(index_a))
    order_blocks = np.argsort(ranks[:, 0])
    runs = tuple(strided(ranks[order_blocks, n]) for n in range(blocks_b))

    modes_z = modes(np.arange(cells), cells - np.arange(cells), cells, length)
    tz_back = halves((weights * modes_z)[per_c * index_b + index_a])
    sub, owner = np.divmod(np.arange(cells), blocks_a)
    order_b = np.where(owner < blocks_a // 2, per_b * owner + sub, length - 1 - per_b * owner - sub)
    modes_y = modes(order_b, np.where(order_b == 0, cells, order_b), cells, length)
    ty, ty_back = halves(modes_y.T), halves(weights * modes_y)
    order_a = np.arange(cells)
    modes_x = modes(order_a, np.where(order_a == 0, cells, order_a), cells, length)
    order_x = np.arange(cells).reshape(blocks_a, slab_x).T
    tx = halves(modes_x[:, order_x.reshape(-1)])
    tx_back = halves((weights * modes_x)[:, order_x[:, order_blocks].reshape(-1)].T)

    rows, tiles = cells // blocks_a, cells // 128
    total = blocks_b + rows * tiles + 2
    places = dict(blocks_a=blocks_a, blocks_b=blocks_b, slab_x=slab_x, slab_y=slab_y)

    sent = call(forward_z, (length, slab_x * slab_y), (density,), 10**9)
    got = lax.all_to_all(sent, COL, split_axis=0, concat_axis=0, tiled=True)
    packed = call(functools.partial(pack, **places), (blocks_a * total, 128), (got, kernel_hat), 0)
    got = lax.all_to_all(packed.reshape(blocks_a, 1, total * 128), GA, split_axis=0, concat_axis=0, tiled=True)
    back = call(
        functools.partial(convolve, runs=runs, **places),
        (length, slab_x * slab_y),
        (got.reshape(blocks_a * total, 128), ty, tx, ty_back, tx_back),
        6 * 200 * 10**6,
    )
    got = lax.all_to_all(back, RANKS, split_axis=0, concat_axis=0, tiled=True)
    return call(inverse_z, density.shape, (got, tz_back), 6 * 128 * 256 * 512)


def solution(mesh):
    devices = mesh.devices
    grp, row, col = devices.shape
    parts = Mesh(devices.reshape(grp, row // 2, 2, 2, col // 2), ("grp", "ra", "rb", "ca", "cb"))
    return jax.shard_map(
        body,
        mesh=parts,
        in_specs=(P(GA, COL, None), P(GA, COL, None)),
        out_specs=P(GA, COL, None),
        check_vma=False,
    )
```

```python
import functools
import math

import jax
import jax.numpy as jnp
import ml_dtypes
import numpy as np
from jax import lax
from jax.experimental import pallas as pl
from jax.experimental.pallas import tpu as pltpu
from jax.sharding import Mesh
from jax.sharding import PartitionSpec as P


GA = ("grp", "ra", "rb")
COL = ("ca", "cb")
RANKS = ("grp", "ra", "cb", "ca", "rb")
NN = (((1,), (0,)), ((), ()))
NT = (((1,), (1,)), ((), ()))
TN = (((0,), (0,)), ((), ()))
VMEM = pl.BlockSpec(memory_space=pltpu.VMEM)


def modes(freqs_c, freqs_s, cells, length):
    centre = np.arange(cells) - (cells - 1) / 2.0
    angle = 2.0 * np.pi / length
    return np.concatenate(
        [np.cos(angle * np.outer(freqs_c, centre)), np.sin(angle * np.outer(freqs_s, centre))], 0
    )


def halves(table):
    table = np.asarray(table, np.float32)
    hi = table.astype(ml_dtypes.bfloat16)
    lo = (table - hi.astype(np.float32)).astype(ml_dtypes.bfloat16)
    return jnp.asarray(np.stack([hi, lo]))


def split(x):
    hi = x.astype(jnp.bfloat16)
    return hi, (x - hi.astype(jnp.float32)).astype(jnp.bfloat16)


def dot3(left, right, dims):
    one = functools.partial(lax.dot_general, dimension_numbers=dims, preferred_element_type=jnp.float32)
    return one(left[0], right[0]) + (one(left[0], right[1]) + one(left[1], right[0]))


def exchange_blocks(v, block):
    count, lanes = len(v), v[0].shape[1]
    lane_block = lax.broadcasted_iota(jnp.int32, v[0].shape, 1) // block
    step = 1
    while step < count:
        odd = (lane_block & step) != 0
        w = list(v)
        for n in range(count):
            if n & step == 0:
                low, high = v[n], v[n + step]
                w[n] = jnp.where(odd, pltpu.roll(high, step * block, 1), low)
                w[n + step] = jnp.where(odd, high, pltpu.roll(low, lanes - step * block, 1))
        v = w
        step *= 2
    return v


def table_z(length, cells, step=16):
    def pair(rows, scale):
        n = lax.broadcasted_iota(jnp.int32, (rows, cells), 0) * scale
        offset = 2 * lax.broadcasted_iota(jnp.int32, (rows, cells), 1) - (cells - 1)
        turn = lax.rem(n * offset, 2 * length)
        angle = turn.astype(jnp.float32) * (math.pi / length)
        return jnp.cos(angle), jnp.sin(angle)

    cos_u, sin_u = pair(length // step, step)
    cos_v, sin_v = pair(step, 1)
    blocks = []
    for u in range(length // step):
        c, s = cos_u[u : u + 1], sin_u[u : u + 1]
        blocks.append(c * cos_v - s * sin_v if 2 * u * step < length else s * cos_v + c * sin_v)
    return jnp.concatenate(blocks, 0)


def forward_z(d_ref, out_ref):
    d = d_ref[...]
    d = d.reshape(d.shape[0] * d.shape[1], d.shape[2])
    out_ref[...] = dot3(split(table_z(out_ref.shape[0], d.shape[1])), split(d), NT)


def pack(r_ref, k_ref, out_ref, *, blocks_a, blocks_b, slab_x, slab_y):
    half = blocks_b * slab_y
    rows, tiles = half // blocks_a, half // 128
    total = out_ref.shape[0] // blocks_a

    def put(t, value):
        out_ref[pl.ds(t, blocks_a, stride=total), :] = value

    for h in range(blocks_b // slab_x):
        first = h * slab_x * blocks_a
        v = [r_ref[first + n * blocks_a : first + (n + 1) * blocks_a, :] for n in range(slab_x)]
        v = exchange_blocks(v, slab_y)
        for n in range(slab_x):
            put(h * slab_x + n, v[n])
    first = lax.axis_index("grp")
    edge = jnp.logical_and(first == 1, lax.axis_index("ra") + lax.axis_index("rb") == 0)
    lane = lax.broadcasted_iota(jnp.int32, (blocks_a, 128), 1)
    last = pltpu.roll(k_ref[0, :, half : half + 128], rows, 1)
    end = half - 128
    for s in range(rows):
        for h in range(tiles):
            tile = k_ref[first + s, :, h * 128 : (h + 1) * 128]
            if s == rows - 1 and h == tiles - 1:
                tile = jnp.where(edge, k_ref[0, :, end:half], tile)
            put(blocks_b + s * tiles + h, tile)
        column = k_ref[first + s, :, half : half + 128]
        last = jnp.where(lane == s, pltpu.roll(column, s, 1) if s else column, last)
    put(blocks_b + rows * tiles, jnp.where(edge, k_ref[0, :, :128], k_ref[rows, :, end:half]))
    put(blocks_b + rows * tiles + 1, last)


def convolve(r_ref, y_ref, x_ref, y_back_ref, x_back_ref, out_ref, *, blocks_a, blocks_b, slab_x, slab_y, runs):
    half = blocks_b * slab_y
    rows, tiles = half // blocks_a, half // 128
    total = r_ref.shape[0] // blocks_a
    per = slab_x

    def take(t):
        return r_ref[pl.ds(t, blocks_a, stride=total), :]

    r = jnp.concatenate(
        [jnp.concatenate([take(h * per + n) for n in range(per)], 0) for h in range(blocks_b // per)], 1
    )
    p = split(dot3(split(r), (y_ref[0], y_ref[1]), NN))
    q0 = [dot3((x_ref[0, at], x_ref[1, at]), p, NN) for at in (slice(0, half), slice(half, 2 * half))]
    spare, middle = blocks_b + rows * tiles, blocks_a // 2

    def kernel_tile(s, h):
        tile = take(blocks_b + s * tiles + h)
        if s == rows - 1 and h == tiles - 1:
            at = (middle - 1) * total + spare
            owner = lax.broadcasted_iota(jnp.int32, tile.shape, 0)
            tile = jnp.where(owner == middle, r_ref[at : at + 1, :], tile)
        return tile

    main = jnp.concatenate(
        [jnp.concatenate([kernel_tile(s, h) for s in range(rows)], 0).T for h in range(tiles)], 0
    )
    tail = take(spare + 1).T
    line = jnp.concatenate([tail[s : s + 1] for s in range(rows)], 1)
    at = middle * total + spare
    column = jnp.concatenate(
        [jnp.broadcast_to(r_ref[n : n + 1, :], (8, 128)).T[:, :1] for n in (at, at - 1)], 0
    )
    corner = r_ref[at + 1 : at + 2, rows : rows + 1]
    first_row = lax.broadcasted_iota(jnp.int32, main.shape, 0) == 0
    first_lane = lax.broadcasted_iota(jnp.int32, main.shape, 1) == 0
    lined = jnp.where(first_row, line, main)
    with_column = jnp.where(first_row, corner, column)
    kernels = (
        jnp.concatenate([main, jnp.where(first_lane, column, main)], 1),
        jnp.concatenate([lined, jnp.where(first_lane, with_column, lined)], 1),
    )
    y_back = (y_back_ref[0], y_back_ref[1])
    u = []
    for part in range(2):
        u.append(dot3(split(q0[part] * kernels[part]), y_back, NN))
    v = dot3((x_back_ref[0], x_back_ref[1]), split(jnp.concatenate(u, 0)), NN)
    for h in range(blocks_b // per):
        lanes = slice(h * per * slab_y, (h + 1) * per * slab_y)
        v_h = exchange_blocks([v[n * blocks_a : (n + 1) * blocks_a, lanes] for n in range(per)], slab_y)
        for n in range(per):
            done = 0
            for start, step, count in runs[h * per + n]:
                out_ref[pl.ds(start, count, stride=step), :] = v_h[n][done : done + count]
                done += count


def inverse_z(r_ref, t_ref, out_ref):
    out = dot3(split(r_ref[...]), (t_ref[0], t_ref[1]), TN)
    out_ref[...] = out.reshape(out_ref.shape)


def strided(values):
    runs, at = [], 0
    while at < len(values):
        step = values[at + 1] - values[at] if at + 1 < len(values) else 1
        count = 1
        while at + count < len(values) and values[at + count] - values[at + count - 1] == step:
            count += 1
        runs.append((int(values[at]), int(step), count))
        at += count
    return tuple(runs)


def call(kernel, shape, operands, flops):
    size = sum(x.size * x.dtype.itemsize for x in operands) + 4 * int(np.prod(shape))
    return pl.pallas_call(
        kernel,
        out_shape=jax.ShapeDtypeStruct(shape, jnp.float32),
        in_specs=[VMEM] * len(operands),
        out_specs=VMEM,
        compiler_params=pltpu.CompilerParams(vmem_limit_bytes=40 * 1024 * 1024),
        cost_estimate=pl.CostEstimate(flops=flops, bytes_accessed=size, transcendentals=0),
    )(*operands)


def body(density, kernel_hat):
    blocks_a = lax.axis_size(GA)
    blocks_b = lax.axis_size(COL)
    slab_x, slab_y, cells = density.shape
    length = 2 * cells
    per_b, per_c = kernel_hat.shape[:2]
    weights = np.full((2, cells), 2.0 / length)
    weights[:, 0] = 1.0 / length
    weights = weights.reshape(length, 1)

    sizes = {name: lax.axis_size(name) for name in RANKS}
    where = dict(zip(RANKS, np.indices(tuple(sizes.values())).reshape(len(RANKS), -1)))
    index_a = np.ravel_multi_index([where[n] for n in GA], [sizes[n] for n in GA])
    index_b = np.ravel_multi_index([where[n] for n in COL], [sizes[n] for n in COL])
    ranks = np.empty((blocks_a, blocks_b), np.int64)
    ranks[index_a, index_b] = np.arange(len(index_a))
    order_blocks = np.argsort(ranks[:, 0])
    runs = tuple(strided(ranks[order_blocks, n]) for n in range(blocks_b))

    modes_z = modes(np.arange(cells), cells - np.arange(cells), cells, length)
    tz_back = halves((weights * modes_z)[per_c * index_b + index_a])
    sub, owner = np.divmod(np.arange(cells), blocks_a)
    order_b = np.where(owner < blocks_a // 2, per_b * owner + sub, length - 1 - per_b * owner - sub)
    modes_y = modes(order_b, np.where(order_b == 0, cells, order_b), cells, length)
    ty, ty_back = halves(modes_y.T), halves(weights * modes_y)
    order_a = np.arange(cells)
    modes_x = modes(order_a, np.where(order_a == 0, cells, order_a), cells, length)
    order_x = np.arange(cells).reshape(blocks_a, slab_x).T
    tx = halves(modes_x[:, order_x.reshape(-1)])
    tx_back = halves((weights * modes_x)[:, order_x[:, order_blocks].reshape(-1)].T)

    rows, tiles = cells // blocks_a, cells // 128
    total = blocks_b + rows * tiles + 2
    places = dict(blocks_a=blocks_a, blocks_b=blocks_b, slab_x=slab_x, slab_y=slab_y)

    sent = call(forward_z, (length, slab_x * slab_y), (density,), 10**9)
    got = lax.all_to_all(sent, COL, split_axis=0, concat_axis=0, tiled=True)
    packed = call(functools.partial(pack, **places), (blocks_a * total, 128), (got, kernel_hat), 0)
    got = lax.all_to_all(packed.reshape(blocks_a, 1, total * 128), GA, split_axis=0, concat_axis=0, tiled=True)
    back = call(
        functools.partial(convolve, runs=runs, **places),
        (length, slab_x * slab_y),
        (got.reshape(blocks_a * total, 128), ty, tx, ty_back, tx_back),
        6 * 200 * 10**6,
    )
    got = lax.all_to_all(back, RANKS, split_axis=0, concat_axis=0, tiled=True)
    return call(inverse_z, density.shape, (got, tz_back), 6 * 128 * 256 * 512)


def solution(mesh):
    devices = mesh.devices
    grp, row, col = devices.shape
    parts = Mesh(devices.reshape(grp, row // 2, 2, 2, col // 2), ("grp", "ra", "rb", "ca", "cb"))
    return jax.shard_map(
        body,
        mesh=parts,
        in_specs=(P(GA, COL, None), P(GA, COL, None)),
        out_specs=P(GA, COL, None),
        check_vma=False,
    )
```

```python
import functools
import math

import jax
import jax.numpy as jnp
import ml_dtypes
import numpy as np
from jax import lax
from jax.experimental import pallas as pl
from jax.experimental.pallas import tpu as pltpu
from jax.sharding import Mesh
from jax.sharding import PartitionSpec as P


GA = ("grp", "ra", "rb")
COL = ("ca", "cb")
RANKS = ("cb", "ra", "ca", "rb", "grp")
NN = (((1,), (0,)), ((), ()))
NT = (((1,), (1,)), ((), ()))
VMEM = pl.BlockSpec(memory_space=pltpu.VMEM)


def modes(freqs_c, freqs_s, cells, length):
    centre = np.arange(cells) - (cells - 1) / 2.0
    angle = 2.0 * np.pi / length
    return np.concatenate(
        [np.cos(angle * np.outer(freqs_c, centre)), np.sin(angle * np.outer(freqs_s, centre))], 0
    )


def halves(table):
    table = np.asarray(table, np.float32)
    hi = table.astype(ml_dtypes.bfloat16)
    lo = (table - hi.astype(np.float32)).astype(ml_dtypes.bfloat16)
    return jnp.asarray(np.stack([hi, lo]))


def split(x):
    hi = x.astype(jnp.bfloat16)
    return hi, (x - hi.astype(jnp.float32)).astype(jnp.bfloat16)


def dot3(left, right, dims):
    one = functools.partial(lax.dot_general, dimension_numbers=dims, preferred_element_type=jnp.float32)
    return one(left[0], right[0]) + (one(left[0], right[1]) + one(left[1], right[0]))


def exchange_blocks(v, block):
    count, lanes = len(v), v[0].shape[1]
    lane_block = lax.broadcasted_iota(jnp.int32, v[0].shape, 1) // block
    step = 1
    while step < count:
        odd = (lane_block & step) != 0
        w = list(v)
        for n in range(count):
            if n & step == 0:
                low, high = v[n], v[n + step]
                w[n] = jnp.where(odd, pltpu.roll(high, step * block, 1), low)
                w[n + step] = jnp.where(odd, high, pltpu.roll(low, lanes - step * block, 1))
        v = w
        step *= 2
    return v


def table_z(length, cells, step=16):
    def pair(rows, scale):
        n = lax.broadcasted_iota(jnp.int32, (rows, cells), 0) * scale
        offset = 2 * lax.broadcasted_iota(jnp.int32, (rows, cells), 1) - (cells - 1)
        turn = lax.rem(n * offset, 2 * length)
        angle = turn.astype(jnp.float32) * (math.pi / length)
        return jnp.cos(angle), jnp.sin(angle)

    cos_u, sin_u = pair(length // step, step)
    cos_v, sin_v = pair(step, 1)
    blocks = []
    for u in range(length // step):
        c, s = cos_u[u : u + 1], sin_u[u : u + 1]
        blocks.append(c * cos_v - s * sin_v if 2 * u * step < length else s * cos_v + c * sin_v)
    return jnp.concatenate(blocks, 0)


def forward_z(d_ref, out_ref):
    d = d_ref[...]
    d = d.reshape(d.shape[0] * d.shape[1], d.shape[2])
    out_ref[...] = dot3(split(table_z(out_ref.shape[0], d.shape[1])), split(d), NT)


def pack(r_ref, k_ref, out_ref, *, blocks_a, blocks_b, slab_x, slab_y):
    half = blocks_b * slab_y
    rows, tiles = half // blocks_a, half // 128
    total = out_ref.shape[0] // blocks_a

    def put(t, value):
        out_ref[pl.ds(t, blocks_a, stride=total), :] = value

    for h in range(blocks_b // slab_x):
        first = h * slab_x * blocks_a
        v = [r_ref[first + n * blocks_a : first + (n + 1) * blocks_a, :] for n in range(slab_x)]
        v = exchange_blocks(v, slab_y)
        for n in range(slab_x):
            put(h * slab_x + n, v[n])
    first = lax.axis_index("grp")
    edge = jnp.logical_and(first == 1, lax.axis_index("ra") + lax.axis_index("rb") == 0)
    lane = lax.broadcasted_iota(jnp.int32, (blocks_a, 128), 1)
    last = pltpu.roll(k_ref[0, :, half : half + 128], rows, 1)
    end = half - 128
    for s in range(rows):
        for h in range(tiles):
            tile = k_ref[first + s, :, h * 128 : (h + 1) * 128]
            if s == rows - 1 and h == tiles - 1:
                tile = jnp.where(edge, k_ref[0, :, end:half], tile)
            put(blocks_b + s * tiles + h, tile)
        column = k_ref[first + s, :, half : half + 128]
        last = jnp.where(lane == s, pltpu.roll(column, s, 1) if s else column, last)
    put(blocks_b + rows * tiles, jnp.where(edge, k_ref[0, :, :128], k_ref[rows, :, end:half]))
    put(blocks_b + rows * tiles + 1, last)


def convolve(r_ref, y_ref, x_ref, y_back_ref, x_back_ref, out_ref, *, blocks_a, blocks_b, slab_x, slab_y, runs):
    half = blocks_b * slab_y
    rows, tiles = half // blocks_a, half // 128
    total = r_ref.shape[0] // blocks_a
    per = slab_x

    def take(t):
        return r_ref[pl.ds(t, blocks_a, stride=total), :]

    r = jnp.concatenate(
        [jnp.concatenate([take(h * per + n) for n in range(per)], 0) for h in range(blocks_b // per)], 1
    )
    p = split(dot3(split(r), (y_ref[0], y_ref[1]), NN))
    q0 = [dot3((x_ref[0, at], x_ref[1, at]), p, NN) for at in (slice(0, half), slice(half, 2 * half))]
    spare, middle = blocks_b + rows * tiles, blocks_a // 2

    def kernel_tile(s, h):
        tile = take(blocks_b + s * tiles + h)
        if s == rows - 1 and h == tiles - 1:
            at = (middle - 1) * total + spare
            owner = lax.broadcasted_iota(jnp.int32, tile.shape, 0)
            tile = jnp.where(owner == middle, r_ref[at : at + 1, :], tile)
        return tile

    main = jnp.concatenate(
        [jnp.concatenate([kernel_tile(s, h) for s in range(rows)], 0).T for h in range(tiles)], 0
    )
    tail = take(spare + 1).T
    line = jnp.concatenate([tail[s : s + 1] for s in range(rows)], 1)
    at = middle * total + spare
    column = jnp.concatenate(
        [jnp.broadcast_to(r_ref[n : n + 1, :], (8, 128)).T[:, :1] for n in (at, at - 1)], 0
    )
    corner = r_ref[at + 1 : at + 2, rows : rows + 1]
    first_row = lax.broadcasted_iota(jnp.int32, main.shape, 0) == 0
    first_lane = lax.broadcasted_iota(jnp.int32, main.shape, 1) == 0
    lined = jnp.where(first_row, line, main)
    with_column = jnp.where(first_row, corner, column)
    kernels = (
        jnp.concatenate([main, jnp.where(first_lane, column, main)], 1),
        jnp.concatenate([lined, jnp.where(first_lane, with_column, lined)], 1),
    )
    y_back = (y_back_ref[0], y_back_ref[1])
    u = []
    for part in range(2):
        u.append(dot3(split(q0[part] * kernels[part]), y_back, NN))
    v = dot3((x_back_ref[0], x_back_ref[1]), split(jnp.concatenate(u, 0)), NN)
    for h in range(blocks_b // per):
        lanes = slice(h * per * slab_y, (h + 1) * per * slab_y)
        v_h = exchange_blocks([v[n * blocks_a : (n + 1) * blocks_a, lanes] for n in range(per)], slab_y)
        for n in range(per):
            done = 0
            for start, step, count in runs[h * per + n]:
                out_ref[pl.ds(start, count, stride=step), :] = v_h[n][done : done + count]
                done += count


def inverse_z(r_ref, t_ref, out_ref):
    out = dot3(split(r_ref[...].T), (t_ref[0], t_ref[1]), NN)
    out_ref[...] = out.reshape(out_ref.shape)


def strided(values):
    runs, at = [], 0
    while at < len(values):
        step = values[at + 1] - values[at] if at + 1 < len(values) else 1
        count = 1
        while at + count < len(values) and values[at + count] - values[at + count - 1] == step:
            count += 1
        runs.append((int(values[at]), int(step), count))
        at += count
    return tuple(runs)


def call(kernel, shape, operands, flops):
    size = sum(x.size * x.dtype.itemsize for x in operands) + 4 * int(np.prod(shape))
    return pl.pallas_call(
        kernel,
        out_shape=jax.ShapeDtypeStruct(shape, jnp.float32),
        in_specs=[VMEM] * len(operands),
        out_specs=VMEM,
        compiler_params=pltpu.CompilerParams(vmem_limit_bytes=40 * 1024 * 1024),
        cost_estimate=pl.CostEstimate(flops=flops, bytes_accessed=size, transcendentals=0),
    )(*operands)


def body(density, kernel_hat):
    blocks_a = lax.axis_size(GA)
    blocks_b = lax.axis_size(COL)
    slab_x, slab_y, cells = density.shape
    length = 2 * cells
    per_b, per_c = kernel_hat.shape[:2]
    weights = np.full((2, cells), 2.0 / length)
    weights[:, 0] = 1.0 / length
    weights = weights.reshape(length, 1)

    sizes = {name: lax.axis_size(name) for name in RANKS}
    where = dict(zip(RANKS, np.indices(tuple(sizes.values())).reshape(len(RANKS), -1)))
    index_a = np.ravel_multi_index([where[n] for n in GA], [sizes[n] for n in GA])
    index_b = np.ravel_multi_index([where[n] for n in COL], [sizes[n] for n in COL])
    ranks = np.empty((blocks_a, blocks_b), np.int64)
    ranks[index_a, index_b] = np.arange(len(index_a))
    order_blocks = np.argsort(ranks[:, 0])
    runs = tuple(strided(ranks[order_blocks, n]) for n in range(blocks_b))

    modes_z = modes(np.arange(cells), cells - np.arange(cells), cells, length)
    tz_back = halves((weights * modes_z)[per_c * index_b + index_a])
    sub, owner = np.divmod(np.arange(cells), blocks_a)
    order_b = np.where(owner < blocks_a // 2, per_b * owner + sub, length - 1 - per_b * owner - sub)
    modes_y = modes(order_b, np.where(order_b == 0, cells, order_b), cells, length)
    ty, ty_back = halves(modes_y.T), halves(weights * modes_y)
    order_a = np.arange(cells)
    modes_x = modes(order_a, np.where(order_a == 0, cells, order_a), cells, length)
    order_x = np.arange(cells).reshape(blocks_a, slab_x).T
    tx = halves(modes_x[:, order_x.reshape(-1)])
    tx_back = halves((weights * modes_x)[:, order_x[:, order_blocks].reshape(-1)].T)

    rows, tiles = cells // blocks_a, cells // 128
    total = blocks_b + rows * tiles + 2
    places = dict(blocks_a=blocks_a, blocks_b=blocks_b, slab_x=slab_x, slab_y=slab_y)

    sent = call(forward_z, (length, slab_x * slab_y), (density,), 10**9)
    got = lax.all_to_all(sent, COL, split_axis=0, concat_axis=0, tiled=True)
    packed = call(functools.partial(pack, **places), (blocks_a * total, 128), (got, kernel_hat), 0)
    got = lax.all_to_all(packed.reshape(blocks_a, 1, total * 128), GA, split_axis=0, concat_axis=0, tiled=True)
    back = call(
        functools.partial(convolve, runs=runs, **places),
        (length, slab_x * slab_y),
        (got.reshape(blocks_a * total, 128), ty, tx, ty_back, tx_back),
        6 * 200 * 10**6,
    )
    got = lax.all_to_all(back, RANKS, split_axis=0, concat_axis=0, tiled=True)
    return call(inverse_z, density.shape, (got, tz_back), 6 * 128 * 256 * 512)


def solution(mesh):
    devices = mesh.devices
    grp, row, col = devices.shape
    parts = Mesh(devices.reshape(grp, row // 2, 2, 2, col // 2), ("grp", "ra", "rb", "ca", "cb"))
    return jax.shard_map(
        body,
        mesh=parts,
        in_specs=(P(GA, COL, None), P(GA, COL, None)),
        out_specs=P(GA, COL, None),
        check_vma=False,
    )
```
